128 devices in a mesh: seq: 8 (over z, core), exp: 16 (over y, x).
Axes of the slice: x: 4, y: 4, z: 4, core: 2. Of those that a mesh axis runs over, the one named last changes fastest.
Arguments:
- queries: bfloat16 [16, 1024, 12288], P('exp', 'seq'), may hold values from -16 to 16
- latents: bfloat16 [16, 1024, 576], P('exp', 'seq'), may hold values from -6 to 6
- latent_gain: float32 [512], replicated, may hold values from 0.5 to 1.5
- latent_up: bfloat16 [512, 16384], P(None, 'seq'), may hold values from -0.25 to 0.25
- document_ids: int32 [16, 1024], P('exp', 'seq'), may hold values from 0 to 7, never falling along the last dimension, each value on 1 to 512 neighbouring positions
- output_weights: bfloat16 [8192, 5120], P('seq'), may hold values from -0.0625 to 0.0625
- residual: bfloat16 [16, 1024, 5120], P('exp', 'seq'), may hold values from -6 to 6
- norm_gain: float32 [5120], replicated, may hold values from 0.1 to 1.9
- expert_ids: int32 [16, 1024, 6], P('exp', 'seq'), may hold values from 0 to 159, as said below
- route_gates: float32 [16, 1024, 6], P('exp', 'seq'), may hold values from 0.05 to 0.6
- gate_weights: bfloat16 [16, 1536, 5120], P('exp', 'seq'), may hold values from -0.078125 to 0.078125
- up_weights: bfloat16 [16, 1536, 5120], P('exp', 'seq'), may hold values from -0.078125 to 0.078125
- down_weights: bfloat16 [16, 1536, 5120], P('exp', 'seq'), may hold values from -0.15625 to 0.15625
Outputs:
- layer_output: bfloat16 [16, 1024, 5120], P('exp', 'seq')
The draws below stay inside these ranges and needn't reach their ends.
Inputs may be any that keep to these rules, and one draw needn't show every extreme that they name: `expert_ids`: each row names six different experts, two from each of three different groups (group of an id = id // 10). In each aligned block of 128 rows (the rows of one device) at most 8 rows name any one group's window expert g * 10; in every draw one group's window expert is named by exactly 8 rows in every block.
All inputs are finite; a program needn't handle non-finite values.
Results may differ from the reference program's by a relative error of at most 0.015.
Values may be sent and summed in bfloat16 or wider, within the bound.
No kernel may reach another device: no remote copies, remote signals or barrier semaphores. Data moves between devices by JAX's collectives and lax.ppermute only.
A program may use at most 128 MiB of HBM per device.

```python
import math
import jax
import jax.numpy as jnp
import numpy as np
from jax import lax

D = 5120
HEADS = 64
NOPE = 128
ROPE = 64
VDIM = 128
KV_RANK = 512
FF = 1536
GROUP_EXPERTS = 10
TOP = 6
TOK_DEV = 128
SEQS = 16
LENGTH = 1024
GROUPS = 16
CAP = 8
HG = 8
FFD = 192
N_SEQ = 8


def draw_queries(key, part):
    key = jax.random.fold_in(key, 5)
    base_key = jax.random.fold_in(key, 0)
    block_shape = (SEQS, LENGTH, HEADS * (NOPE + ROPE))
    base = jax.random.normal(base_key, block_shape, jnp.float32)
    return jnp.clip(base, -6.0, 6.0).astype(jnp.bfloat16)


def draw_latents(key, part):
    key = jax.random.fold_in(key, 7)
    base = jax.random.normal(key, (SEQS, LENGTH, KV_RANK + ROPE), jnp.float32)
    base = jnp.clip(base, -6.0, 6.0)
    return base.astype(jnp.bfloat16)


def draw_expert_ids(key, part):
    key = jax.random.fold_in(key, 11)
    subkeys = jax.random.split(key, 9)
    blocks = LENGTH // TOK_DEV
    block_shape = (SEQS, blocks, TOK_DEV)
    score_noise = jax.random.randint(subkeys[0], block_shape + (GROUPS,), 0, 1000)
    favour = jax.random.randint(subkeys[1], (GROUPS,), 0, 1500)
    hottest = jax.random.randint(subkeys[2], (), 0, GROUPS)
    tickets = jax.random.randint(subkeys[3], block_shape, 0, 1 << 20) * TOK_DEV + jnp.arange(TOK_DEV, dtype=jnp.int32)
    placing = jnp.argsort(jnp.argsort(tickets, axis=-1), axis=-1)
    forced = placing < CAP
    labels = jnp.arange(GROUPS, dtype=jnp.int32)
    hot_label = labels == hottest
    group_score = score_noise + favour + jnp.where(forced[..., None] & hot_label, 100000, 0)
    group_score = group_score * GROUPS + labels
    picked = lax.top_k(group_score, 3)[1].astype(jnp.int32)
    window_flags = jax.random.randint(subkeys[4], block_shape + (3,), 0, 20) < 3
    first_slot = jnp.arange(3) == 0
    hot_pick = picked == hottest
    window_flags = jnp.where(hot_pick, forced[..., None] & first_slot, window_flags)
    member = (picked[..., None] == labels) & window_flags[..., None]
    wanted = jnp.any(member, axis=3).astype(jnp.int32)
    before = jnp.cumsum(wanted, axis=2) - wanted
    within_cap = (wanted == 1) & (before < CAP)
    window_flags = window_flags & jnp.take_along_axis(within_cap, picked, axis=3)
    companion = jax.random.randint(subkeys[5], block_shape + (3,), 1, GROUP_EXPERTS)
    offset_draw = jax.random.randint(subkeys[6], block_shape + (3,), 1, GROUP_EXPERTS - 1)
    spare_expert = 1 + (companion - 1 + offset_draw) % (GROUP_EXPERTS - 1)
    lead_expert = jnp.where(window_flags, 0, spare_expert)
    swapped = jax.random.randint(subkeys[7], block_shape + (3,), 0, 2) == 1
    pair_first = jnp.where(swapped, companion, lead_expert)
    pair_second = jnp.where(swapped, lead_expert, companion)
    route_ids = picked[..., None] * GROUP_EXPERTS + jnp.stack([pair_first, pair_second], axis=-1)
    rotation = jax.random.randint(subkeys[8], block_shape + (1,), 0, 3)
    group_order = (jnp.arange(3, dtype=jnp.int32) + rotation) % 3
    group_order = jnp.broadcast_to(group_order[..., None], route_ids.shape)
    route_ids = jnp.take_along_axis(route_ids, group_order, axis=3)
    return route_ids.reshape(SEQS, LENGTH, TOP).astype(jnp.int32)


def block_scale(own_key, dims, cuts, smallest, high):
    def one(dim, parts):
        steps = jax.random.uniform(jax.random.fold_in(jax.random.fold_in(own_key, 6), dim), (parts,), jnp.float32, smallest / len(cuts), high / len(cuts))
        return jnp.repeat(jnp.exp(steps), dims[dim] // parts).reshape((-1,) + (1,) * (len(dims) - dim - 1))

    level = one(*cuts[0])
    for cut in cuts[1:]:
        level = level * one(*cut)
    return level


def length_profile(number_of, total, reach, lean):
    loads = [(1 << 20) // math.isqrt(rank ** lean) + 1 for rank in range(2, number_of + 1)]
    surplus, counts = total - reach - (number_of - 1), [1] * (number_of - 1)
    while surplus > 0:
        movable = [i for i in range(number_of - 1) if counts[i] < reach]
        mass, budget = sum([loads[i] for i in movable]), surplus
        for i in movable:
            extra = min(reach - counts[i], max(1, budget * loads[i] // mass), surplus)
            counts[i] = counts[i] + extra
            surplus = surplus - extra
    return np.array([reach] + counts)


def uneven_parts(key, amount, total, most, slope):
    if amount == 2:
        one = jax.random.randint(key, (), max(1, total - most), min(most, total - 1) + 1)
        return jnp.stack([one, total - one])
    tallies = jnp.asarray(length_profile(amount, total, most, slope), jnp.int32)
    pairs = (amount - 1) // 2
    source_of, receiver = tallies[1:1 + 2 * pairs:2], tallies[2:2 + 2 * pairs:2]
    margin = jnp.minimum(source_of - 1, most - receiver)
    shifted = jax.random.randint(jax.random.fold_in(key, 1), (pairs,), 0, 1 << 20) % (margin + 1)
    tallies = tallies.at[1:1 + 2 * pairs:2].set(source_of - shifted).at[2:2 + 2 * pairs:2].set(receiver + shifted)
    return tallies[jax.random.permutation(jax.random.fold_in(key, 2), amount)]


def bell_draw(key, extent, scale, most, cuts=(), kind=jnp.bfloat16):
    array = jax.random.normal(key, extent, jnp.float32) * scale
    if len(cuts) > 0:
        array = block_scale(key, extent, cuts, -0.22, 0.18) * array
    return jnp.clip(array, min=-most, max=most).astype(kind)


def setup_inputs(seed: int = 0) -> dict:
    key_of = jax.random.split(jax.random.key(seed), 14)
    queries = draw_queries(jax.random.fold_in(key_of[13], 71), 0)
    latents = draw_latents(jax.random.fold_in(key_of[13], 71), 0)
    latent_gain = jnp.clip(1.0 + 0.1 * jax.random.normal(key_of[2], (KV_RANK,), jnp.float32), 0.5, 1.5)
    latent_up = bell_draw(key_of[3], (KV_RANK, HEADS * (NOPE + VDIM)), KV_RANK ** -0.5, 0.25, ((1, 8),))
    document_ids = jax.vmap(lambda own: jnp.searchsorted(jnp.cumsum(uneven_parts(own, 8, LENGTH, LENGTH // 2, 1)), jnp.arange(LENGTH), side="right"))(jax.random.split(key_of[4], SEQS)).reshape((SEQS, LENGTH)).astype(jnp.int32)
    output_weights = bell_draw(key_of[5], (HEADS * VDIM, D), (HEADS * VDIM) ** -0.5, 0.0625, ((0, 8),))
    residual = bell_draw(key_of[6], (SEQS, LENGTH, D), 1.0, 6.0, ((0, 16), (1, 8)))
    norm_gain = jnp.clip(1.0 + 0.18 * jax.random.normal(key_of[7], (D,), jnp.float32), 0.1, 1.9)
    expert_ids = draw_expert_ids(jax.random.fold_in(key_of[13], 71), 0)
    route_gates = jnp.clip(jnp.exp(math.log(0.6) - 2.4849067 * jax.random.uniform(key_of[9], (SEQS, LENGTH, TOP), jnp.float32) ** block_scale(key_of[9], (SEQS, LENGTH, TOP), ((0, 16), (1, 8)), -0.2, 0.2)), 0.05, 0.6)
    gate_weights = bell_draw(key_of[10], (GROUPS, FF, D), D ** -0.5, 0.078125, ((0, 16), (1, 8)))
    up_weights = bell_draw(key_of[11], (GROUPS, FF, D), D ** -0.5, 0.078125, ((0, 16), (1, 8)))
    down_weights = bell_draw(key_of[12], (GROUPS, FF, D), FF ** -0.5, 0.15625, ((0, 16), (1, 8)))
    return {"queries": queries, "latents": latents, "latent_gain": latent_gain, "latent_up": latent_up, "document_ids": document_ids, "output_weights": output_weights, "residual": residual, "norm_gain": norm_gain, "expert_ids": expert_ids, "route_gates": route_gates, "gate_weights": gate_weights, "up_weights": up_weights, "down_weights": down_weights}


EPS = 1e-06
MASKED = -1e+30

def rms_scale(values, gain):
    mean_sq = lax.optimization_barrier(jnp.mean(values * values, axis=-1, keepdims=True))
    return values * lax.rsqrt(mean_sq + EPS) * gain

def expert_block(source_rows, gate_part, up_part, down_part):
    gate_proj = jnp.dot(source_rows, gate_part.T, preferred_element_type=jnp.float32)
    up_proj = jnp.dot(source_rows, up_part.T, preferred_element_type=jnp.float32)
    active = (jax.nn.silu(gate_proj) * up_proj).astype(jnp.bfloat16)
    running = jnp.zeros((source_rows.shape[0], D), jnp.float32)
    for shard_index in range(N_SEQ):
        bottom = shard_index * FFD
        partial_value = jnp.dot(active[:, bottom:bottom + FFD], down_part[bottom:bottom + FFD], preferred_element_type=jnp.float32)
        partial_value = lax.optimization_barrier(partial_value.astype(jnp.bfloat16))
        running = running + partial_value.astype(jnp.float32)
    return running.astype(jnp.bfloat16)

def attend_sequence(query_seq, latent_seq, docs, latent_gain, latent_up, output_weights):
    head_width = NOPE + VDIM
    query_width = NOPE + ROPE
    normed = rms_scale(latent_seq[:, :KV_RANK].astype(jnp.float32), latent_gain).astype(jnp.bfloat16)
    rope_keys = latent_seq[:, KV_RANK:].astype(jnp.float32)
    key_values = jnp.dot(normed, latent_up, preferred_element_type=jnp.float32).astype(jnp.bfloat16)
    places = jnp.arange(LENGTH, dtype=jnp.int32)
    visible = (places[None, :] <= places[:, None]) & (docs[None, :] == docs[:, None])
    score_scale = query_width ** (-0.5)

    def one_group(running, group_index):
        query_start = (group_index * (HG * query_width)).astype(jnp.int32)
        block_queries = lax.dynamic_slice_in_dim(query_seq, query_start, HG * query_width, 1)
        block_queries = block_queries.astype(jnp.float32).reshape(LENGTH, HG, query_width)
        kv_start = (group_index * (HG * head_width)).astype(jnp.int32)
        block_kv = lax.dynamic_slice_in_dim(key_values, kv_start, HG * head_width, 1)
        block_kv = block_kv.astype(jnp.float32).reshape(LENGTH, HG, head_width)
        scores = jnp.einsum('qhd,khd->hqk', block_queries[:, :, :NOPE], block_kv[:, :, :NOPE])
        scores = scores + jnp.einsum('qhd,kd->hqk', block_queries[:, :, NOPE:], rope_keys)
        scores = jnp.where(visible[None], scores * score_scale, MASKED)
        row_peak = lax.optimization_barrier(jnp.max(scores, axis=-1, keepdims=True))
        weights = jnp.exp(scores - row_peak)
        probability = (weights / lax.optimization_barrier(jnp.sum(weights, axis=-1, keepdims=True))).astype(jnp.bfloat16)
        mixed_heads = jnp.einsum('hqk,khd->qhd', probability.astype(jnp.float32), block_kv[:, :, NOPE:])
        mixed_heads = mixed_heads.astype(jnp.bfloat16).reshape(LENGTH, HG * VDIM)
        row_start = (group_index * (HG * VDIM)).astype(jnp.int32)
        weight_rows = lax.dynamic_slice_in_dim(output_weights, row_start, HG * VDIM, 0)
        partial_value = jnp.dot(mixed_heads, weight_rows, preferred_element_type=jnp.float32)
        partial_value = lax.optimization_barrier(partial_value.astype(jnp.bfloat16))
        return (running + partial_value.astype(jnp.float32), None)
    running, _ = lax.scan(one_group, jnp.zeros((LENGTH, D), jnp.float32), jnp.arange(N_SEQ, dtype=jnp.int32))
    return running

def reference(queries, latents, latent_gain, latent_up, document_ids, output_weights, residual, norm_gain, expert_ids, route_gates, gate_weights, up_weights, down_weights):

    def per_sequence(sequence_items):
        return attend_sequence(sequence_items[0], sequence_items[1], sequence_items[2], latent_gain, latent_up, output_weights)
    attention = lax.map(per_sequence, (queries, latents, document_ids))
    hidden = (residual.astype(jnp.float32) + attention).astype(jnp.bfloat16)
    moe_input = rms_scale(hidden.astype(jnp.float32), norm_gain).astype(jnp.bfloat16)
    blocks = LENGTH // TOK_DEV
    block_grid = (SEQS, blocks, TOK_DEV)
    tokens = moe_input.reshape(block_grid + (D,))
    route_ids = expert_ids.reshape(block_grid + (TOP,))
    gates = route_gates.reshape(block_grid + (TOP,)).astype(jnp.float32)
    window = jnp.arange(GROUPS, dtype=jnp.int32) * GROUP_EXPERTS
    matches = route_ids[..., None] == window
    chosen = jnp.any(matches, axis=3).astype(jnp.int32)
    gate_share = lax.optimization_barrier(jnp.sum(jnp.where(matches, gates[..., None], jnp.zeros((), jnp.float32)), axis=3))
    slot_rank = (jnp.cumsum(chosen, axis=2) - chosen).astype(jnp.int32)
    slot_hit = (chosen[..., None] == 1) & (slot_rank[..., None] == jnp.arange(CAP, dtype=jnp.int32))
    positions = jnp.arange(TOK_DEV, dtype=jnp.int32)[:, None, None]
    source_row = lax.optimization_barrier(jnp.sum(jnp.where(slot_hit, positions, 0), axis=2)).astype(jnp.int32)
    filled = jnp.any(slot_hit, axis=2)
    safe_rank = jnp.minimum(slot_rank, CAP - 1).astype(jnp.int32)
    seq_index = jnp.arange(SEQS, dtype=jnp.int32)[:, None, None]
    blk_index = jnp.arange(blocks, dtype=jnp.int32)[None, :, None]

    def one_group(running, group_index):
        source_rows = jnp.take(source_row, group_index, axis=2)
        live_slots = jnp.take(filled, group_index, axis=2)
        picked = tokens[seq_index, blk_index, source_rows]
        picked = jnp.where(live_slots[..., None], picked, jnp.zeros((), jnp.bfloat16))
        out_rows = expert_block(picked.reshape(-1, D), gate_weights[group_index], up_weights[group_index], down_weights[group_index])
        out_rows = out_rows.reshape(SEQS, blocks, CAP, D)
        returned_rows = out_rows[seq_index, blk_index, jnp.take(safe_rank, group_index, axis=3)]
        group_gate = jnp.take(gate_share, group_index, axis=3)
        return (running + group_gate[..., None] * returned_rows.astype(jnp.float32), None)
    moe_sum, _ = lax.scan(one_group, jnp.zeros(block_grid + (D,), jnp.float32), jnp.arange(GROUPS, dtype=jnp.int32))
    return (hidden.astype(jnp.float32) + moe_sum.reshape(SEQS, LENGTH, D)).astype(jnp.bfloat16)
```

```python
import jax
import jax.numpy as jnp
from jax import lax
from jax.experimental import pallas as pl
from jax.experimental.pallas import tpu as pltpu
from jax.sharding import PartitionSpec as P

NOPE = 128
ROPE = 64
VDIM = 128
KV_RANK = 512
GROUP_EXPERTS = 10
CAP = 8
DOC_MAX = 512
QUERY_BLOCK = 256
PACKED = 640


EPS = 1e-06
MASKED = -1e30
LOG2_E = 1.4426950408889634


def rms_scale(values, gain):
    mean_sq = jnp.mean(values * values, axis=-1, keepdims=True)
    return values * lax.rsqrt(mean_sq + EPS) * gain


def key_windows(length):
    windows = []
    for start in range(0, length, QUERY_BLOCK):
        first = max(0, start - DOC_MAX + 1) // QUERY_BLOCK * QUERY_BLOCK
        windows.append((start, first, start + QUERY_BLOCK))
    return windows


def attend_kernel(windows, q_ref, latent_ref, up_ref, doc_col_ref, doc_row_ref, out_ref, key_ref, value_ref, bias_ref):
    @pl.when(pl.program_id(0) == 0)
    def _():
        for index, (start, first, end) in enumerate(windows):
            shape = (QUERY_BLOCK, end - first)
            query_pos = start + lax.broadcasted_iota(jnp.int32, shape, 0)
            key_pos = first + lax.broadcasted_iota(jnp.int32, shape, 1)
            same = doc_col_ref[start : start + QUERY_BLOCK, :] == doc_row_ref[:, first:end]
            bias_ref[index, :, : end - first] = jnp.where((key_pos <= query_pos) & same, 0.0, MASKED)
        value_ref[:, VDIM : 2 * VDIM] = jnp.ones((value_ref.shape[0], VDIM), jnp.bfloat16)

    key_values = jnp.dot(latent_ref[...], up_ref[0], preferred_element_type=jnp.float32).astype(jnp.bfloat16)
    key_ref[...] = key_values[:, :512]
    value_ref[:, :VDIM] = key_values[:, 512 : 512 + VDIM]
    value_ref[:, 2 * VDIM :] = key_values[:, 512 + VDIM :]
    scale = (NOPE + ROPE) ** (-0.5) * LOG2_E
    for index, (start, first, end) in enumerate(windows):
        for head in range(2):
            queries = q_ref[start : start + QUERY_BLOCK, head * 128 : head * 128 + 256]
            scores = lax.dot_general(
                queries,
                key_ref[first:end, head * 256 : head * 256 + 256],
                (((1,), (1,)), ((), ())),
                preferred_element_type=jnp.float32,
            )
            scores = scores * scale + bias_ref[index, :, : end - first]
            peak = jnp.max(scores, axis=-1, keepdims=True)
            weights = jnp.exp2(scores - peak).astype(jnp.bfloat16)
            mixed = jnp.dot(
                weights, value_ref[first:end, head * 128 : head * 128 + 256], preferred_element_type=jnp.float32
            )
            low, high = mixed[:, :VDIM], mixed[:, VDIM:]
            result = low / high if head == 0 else high / low
            out_ref[start : start + QUERY_BLOCK, head * VDIM : (head + 1) * VDIM] = result.astype(jnp.bfloat16)


def attend(head_queries, latent, up, docs):
    length, width = head_queries.shape
    pairs = width // 384
    windows = key_windows(length)
    widest = max(end - first for _, first, end in windows)
    return pl.pallas_call(
        lambda *refs: attend_kernel(windows, *refs),
        grid=(pairs,),
        out_shape=jax.ShapeDtypeStruct((length, pairs * 256), jnp.bfloat16),
        in_specs=[
            pl.BlockSpec((length, 384), lambda i: (0, i)),
            pl.BlockSpec((length, PACKED), lambda i: (0, 0)),
            pl.BlockSpec((1, PACKED, 768), lambda i: (i, 0, 0)),
            pl.BlockSpec((length, 1), lambda i: (0, 0)),
            pl.BlockSpec((1, length), lambda i: (0, 0)),
        ],
        out_specs=pl.BlockSpec((length, 256), lambda i: (0, i)),
        scratch_shapes=[
            pltpu.VMEM((length, 512), jnp.bfloat16),
            pltpu.VMEM((length, 3 * VDIM), jnp.bfloat16),
            pltpu.VMEM((len(windows), QUERY_BLOCK, widest), jnp.float32),
        ],
        compiler_params=pltpu.CompilerParams(vmem_limit_bytes=40 << 20),
        cost_estimate=pl.CostEstimate(flops=8 * 10**9, bytes_accessed=12 << 20, transcendentals=5 * 10**6),
        name="attend",
    )(head_queries, latent, up, docs[:, None], docs[None, :])


def packed_up(latent_up):
    rank = latent_up.shape[0]
    heads = latent_up.reshape(rank, -1, 2, NOPE + VDIM).transpose(1, 0, 2, 3)
    pairs = heads.shape[0]
    gap = jnp.zeros((pairs, rank, ROPE), jnp.bfloat16)
    top = jnp.concatenate(
        [
            heads[:, :, 0, :NOPE],
            gap,
            gap,
            gap,
            heads[:, :, 1, :NOPE],
            gap,
            heads[:, :, 0, NOPE:],
            heads[:, :, 1, NOPE:],
        ],
        axis=2,
    )
    row = jnp.arange(PACKED - rank)[:, None]
    column = jnp.arange(768)[None, :]
    shared = (row < ROPE) & ((column == row + NOPE) | (column == row + 448))
    bottom = jnp.broadcast_to(shared.astype(jnp.bfloat16), (pairs, PACKED - rank, 768))
    return jnp.concatenate([top, bottom], axis=1)


def expert_kernel(rows_ref, gate_ref, up_ref, down_ref, out_ref):
    rows = rows_ref[...]
    contract = (((1,), (1,)), ((), ()))
    gate_proj = lax.dot_general(rows, gate_ref[...], contract, preferred_element_type=jnp.float32)
    up_proj = lax.dot_general(rows, up_ref[...], contract, preferred_element_type=jnp.float32)
    active = (gate_proj / (1.0 + jnp.exp(-gate_proj)) * up_proj).astype(jnp.bfloat16)
    out_ref[...] = jnp.dot(active, down_ref[...], preferred_element_type=jnp.float32).astype(jnp.bfloat16)


def expert_rows(arrived, gate_part, up_part, down_part):
    count, width = arrived.shape
    tile = 256
    whole = pl.BlockSpec(gate_part.shape, lambda i: (0, 0))
    return pl.pallas_call(
        expert_kernel,
        grid=(count // tile,),
        out_shape=jax.ShapeDtypeStruct((count, width), jnp.bfloat16),
        in_specs=[pl.BlockSpec((tile, width), lambda i: (i, 0)), whole, whole, whole],
        out_specs=pl.BlockSpec((tile, width), lambda i: (i, 0)),
        compiler_params=pltpu.CompilerParams(vmem_limit_bytes=40 << 20),
        cost_estimate=pl.CostEstimate(flops=count * width * 192 * 6, bytes_accessed=28 << 20, transcendentals=count * 192),
        name="expert",
    )(arrived, gate_part, up_part, down_part)


def on_device(
    queries,
    latents,
    latent_gain,
    latent_up,
    document_ids,
    output_weights,
    residual,
    norm_gain,
    expert_ids,
    route_gates,
    gate_weights,
    up_weights,
    down_weights,
):
    seq_count = lax.axis_size("seq")
    group_count = lax.axis_size("exp")
    tok_rows = residual.shape[1]
    model_width = residual.shape[2]
    normed = rms_scale(latents[0, :, :KV_RANK].astype(jnp.float32), latent_gain).astype(
        jnp.bfloat16
    )
    packed = jnp.concatenate(
        [normed, latents[0, :, KV_RANK:], jnp.zeros((tok_rows, PACKED - KV_RANK - ROPE), jnp.bfloat16)], axis=1
    )
    all_latent, all_docs = (
        lax.all_gather(packed, "seq", axis=0, tiled=True),
        lax.all_gather(document_ids[0], "seq", axis=0, tiled=True),
    )
    by_head = jnp.swapaxes(queries[0].reshape(tok_rows, seq_count, -1), 0, 1)
    head_queries = lax.all_to_all(by_head, "seq", split_axis=0, concat_axis=0, tiled=True)
    head_queries = head_queries.reshape(seq_count * tok_rows, -1)
    head_out = attend(head_queries, all_latent, packed_up(latent_up), all_docs)
    attention = lax.psum_scatter(
        jnp.dot(head_out, output_weights, preferred_element_type=jnp.float32).astype(jnp.bfloat16),
        "seq",
        scatter_dimension=0,
        tiled=True,
    ).astype(jnp.float32)
    hidden = (residual[0].astype(jnp.float32) + attention).astype(jnp.bfloat16)
    moe_input = rms_scale(hidden.astype(jnp.float32), norm_gain).astype(jnp.bfloat16)
    window = jnp.arange(group_count, dtype=jnp.int32) * GROUP_EXPERTS
    matches = expert_ids[0][:, :, None] == window
    chosen = jnp.any(matches, axis=1).astype(jnp.bfloat16)
    gate_share = jnp.sum(
        jnp.where(matches, route_gates[0][:, :, None], jnp.zeros((), jnp.float32)), axis=1
    )
    row_ids = jnp.arange(tok_rows, dtype=jnp.int32)
    earlier = (row_ids[None, :] < row_ids[:, None]).astype(jnp.bfloat16)
    slot_rank = jnp.dot(earlier, chosen, preferred_element_type=jnp.float32)
    slot_ids = jnp.arange(CAP, dtype=jnp.float32)
    slot_picks = chosen.astype(jnp.float32)[:, :, None] * (
        slot_rank[:, :, None] == slot_ids
    ).astype(jnp.float32)
    slot_picks = slot_picks.reshape(tok_rows, group_count * CAP)
    outgoing = jnp.einsum(
        "ts,td->sd", slot_picks.astype(jnp.bfloat16), moe_input, preferred_element_type=jnp.float32
    ).astype(jnp.bfloat16)
    arrived = lax.all_to_all(
        outgoing.reshape(group_count, CAP, model_width), "exp", split_axis=0, concat_axis=0, tiled=True
    ).reshape(group_count * CAP, model_width)
    arrived = lax.all_gather(arrived, "seq", axis=0, tiled=True)
    partial_value = expert_rows(arrived, gate_weights[0], up_weights[0], down_weights[0])
    summed = lax.psum_scatter(partial_value, "seq", scatter_dimension=0, tiled=True)
    expert_out = lax.all_to_all(
        summed.reshape(group_count, CAP, model_width), "exp", split_axis=0, concat_axis=0, tiled=True
    ).reshape(group_count * CAP, model_width)
    mixing = slot_picks * jnp.repeat(gate_share, CAP, axis=1)
    moe_sum = jnp.dot(
        mixing,
        expert_out.astype(jnp.float32),
        precision=lax.Precision.HIGHEST,
        preferred_element_type=jnp.float32,
    )
    result = (hidden.astype(jnp.float32) + moe_sum).astype(jnp.bfloat16)
    return result[None]


def solution(mesh):
    return jax.shard_map(
        on_device,
        mesh=mesh,
        in_specs=(
            P("exp", "seq", None),
            P("exp", "seq", None),
            P(),
            P(None, "seq"),
            P("exp", "seq"),
            P("seq", None),
            P("exp", "seq", None),
            P(),
            P("exp", "seq", None),
            P("exp", "seq", None),
            P("exp", "seq", None),
            P("exp", "seq", None),
            P("exp", "seq", None),
        ),
        out_specs=P("exp", "seq", None),
        check_vma=False,
    )
```

```python
import jax
import jax.numpy as jnp
from jax import lax
from jax.experimental import pallas as pl
from jax.experimental.pallas import tpu as pltpu
from jax.sharding import PartitionSpec as P

NOPE = 128
ROPE = 64
VDIM = 128
KV_RANK = 512
GROUP_EXPERTS = 10
CAP = 8
DOC_MAX = 512
QUERY_BLOCK = 256
PACKED = 640
SCOPED = 24 << 20
LARGE = 58 << 20


EPS = 1e-06
MASKED = -1e30
LOG2_E = 1.4426950408889634


def rms_scale(values, gain):
    mean_sq = jnp.mean(values * values, axis=-1, keepdims=True)
    return values * lax.rsqrt(mean_sq + EPS) * gain


def key_windows(length):
    windows = []
    for start in range(0, length, QUERY_BLOCK):
        first = max(0, start - DOC_MAX + 1) // QUERY_BLOCK * QUERY_BLOCK
        windows.append((start, first, start + QUERY_BLOCK))
    return windows


def split_kernel(in_ref, out_ref):
    pieces, _, share = out_ref.shape
    for index in range(pieces):
        out_ref[index] = in_ref[:, index * share : (index + 1) * share]


def split_columns(array, pieces):
    rows, width = array.shape
    share = width // pieces
    some = pieces // 2
    return pl.pallas_call(
        split_kernel,
        grid=(2,),
        in_specs=[pl.BlockSpec((rows, some * share), lambda i: (0, i))],
        out_specs=pl.BlockSpec((some, rows, share), lambda i: (i, 0, 0)),
        out_shape=jax.ShapeDtypeStruct((pieces, rows, share), array.dtype),
        compiler_params=pltpu.CompilerParams(vmem_limit_bytes=SCOPED),
        cost_estimate=pl.CostEstimate(flops=0, bytes_accessed=4 * rows * width, transcendentals=0),
        name="split_columns",
    )(array)


def shared_kernel(latent_ref, up_ref, key_ref, value_ref):
    key_values = jnp.dot(latent_ref[:, :KV_RANK], up_ref[...], preferred_element_type=jnp.float32)
    tail = latent_ref[:, KV_RANK:].astype(jnp.float32)
    tail = jnp.where(lax.broadcasted_iota(jnp.int32, tail.shape, 1) < ROPE, tail, 0.0)
    wide = NOPE + VDIM
    key_ref[:, :256] = jnp.concatenate([key_values[:, :NOPE], tail], axis=1).astype(jnp.bfloat16)
    second = jnp.concatenate([key_values[:, wide : wide + NOPE], tail], axis=1)
    key_ref[:, 256:] = pltpu.roll(second, ROPE, 1).astype(jnp.bfloat16)
    value_ref[:, :VDIM] = key_values[:, NOPE:wide].astype(jnp.bfloat16)
    value_ref[:, VDIM : 2 * VDIM] = jnp.ones((value_ref.shape[0], VDIM), jnp.bfloat16)
    value_ref[:, 2 * VDIM :] = key_values[:, wide + NOPE :].astype(jnp.bfloat16)


def keys_and_values(latent, up):
    length = latent.shape[0]
    pairs = up.shape[1] // 512
    return pl.pallas_call(
        shared_kernel,
        grid=(pairs,),
        out_shape=[
            jax.ShapeDtypeStruct((length, pairs * 512), jnp.bfloat16),
            jax.ShapeDtypeStruct((length, pairs * 384), jnp.bfloat16),
        ],
        in_specs=[
            pl.BlockSpec((length, PACKED), lambda i: (0, 0)),
            pl.BlockSpec((KV_RANK, 512), lambda i: (0, i)),
        ],
        out_specs=[
            pl.BlockSpec((length, 512), lambda i: (0, i)),
            pl.BlockSpec((length, 384), lambda i: (0, i)),
        ],
        compiler_params=pltpu.CompilerParams(vmem_limit_bytes=SCOPED),
        cost_estimate=pl.CostEstimate(flops=2 * length * KV_RANK * 512 * pairs, bytes_accessed=12 << 20, transcendentals=0),
        name="keys_and_values",
    )(latent, up)


def attend_kernel(windows, where_ref, q_ref, key_ref, value_ref, doc_col_ref, doc_row_ref, out_ref, bias_ref):
    @pl.when(pl.program_id(0) == 0)
    def _():
        for index, (start, first, end) in enumerate(windows):
            shape = (QUERY_BLOCK, end - first)
            query_pos = start + lax.broadcasted_iota(jnp.int32, shape, 0)
            key_pos = first + lax.broadcasted_iota(jnp.int32, shape, 1)
            same = doc_col_ref[start : start + QUERY_BLOCK, :] == doc_row_ref[:, first:end]
            bias_ref[index, :, : end - first] = jnp.where((key_pos <= query_pos) & same, 0.0, MASKED)

    scale = (NOPE + ROPE) ** (-0.5) * LOG2_E
    for index, (start, first, end) in enumerate(windows):
        for head in range(2):
            queries = q_ref[start : start + QUERY_BLOCK, head * 128 : head * 128 + 256]
            scores = lax.dot_general(
                queries,
                key_ref[first:end, head * 256 : head * 256 + 256],
                (((1,), (1,)), ((), ())),
                preferred_element_type=jnp.float32,
            )
            scores = scores * scale + bias_ref[index, :, : end - first]
            peak = jnp.max(scores, axis=-1, keepdims=True)
            weights = jnp.exp2(scores - peak).astype(jnp.bfloat16)
            mixed = jnp.dot(
                weights, value_ref[first:end, head * 128 : head * 128 + 256], preferred_element_type=jnp.float32
            )
            low, high = mixed[:, :VDIM], mixed[:, VDIM:]
            result = (low / high if head == 0 else high / low).astype(jnp.bfloat16)
            half = QUERY_BLOCK // 2
            for side in range(2):
                mine = where_ref[0] == side
                turn = 1 - 2 * side
                step = lax.rem((where_ref[1] - index) * turn + 8, 4)
                block = jnp.where(mine, lax.rem(step + 3, 4), 4 + step)
                place = pl.ds(pl.multiple_of(block * half, half), half)
                out_ref[place, head * VDIM : (head + 1) * VDIM] = result[side * half : (side + 1) * half]


def attend(where, head_queries, keys, values, doc_col, doc_row):
    length, width = head_queries.shape
    pairs = width // 384
    windows = key_windows(length)
    widest = max(end - first for _, first, end in windows)
    return pl.pallas_call(
        lambda *refs: attend_kernel(windows, *refs),
        grid_spec=pltpu.PrefetchScalarGridSpec(
            num_scalar_prefetch=1,
            grid=(pairs,),
            in_specs=[
                pl.BlockSpec((length, 384), lambda i, w: (0, i)),
                pl.BlockSpec((length, 512), lambda i, w: (0, i)),
                pl.BlockSpec((length, 384), lambda i, w: (0, i)),
                pl.BlockSpec((length, 1), lambda i, w: (0, 0)),
                pl.BlockSpec((1, length), lambda i, w: (0, 0)),
            ],
            out_specs=pl.BlockSpec((length, 256), lambda i, w: (0, i)),
            scratch_shapes=[pltpu.VMEM((len(windows), QUERY_BLOCK, widest), jnp.float32)],
        ),
        out_shape=jax.ShapeDtypeStruct((length, pairs * 256), jnp.bfloat16),
        compiler_params=pltpu.CompilerParams(vmem_limit_bytes=LARGE),
        cost_estimate=pl.CostEstimate(flops=10**8, bytes_accessed=1 << 20, transcendentals=10**5),
        name="attend",
    )(where, head_queries, keys, values, doc_col, doc_row)


def gate_up_kernel(first, last, width, count, where_ref, *refs):
    blocks = refs[:count]
    gain_ref, gate_ref, up_ref = refs[count : count + 3]
    rest = refs[count + 3 :]
    scaled_ref = rest[-1]
    contract = (((1,), (1,)), ((), ()))
    squares = []
    rows, depth = blocks[0].shape
    for index, parts in enumerate(((blocks[0],), (blocks[1],), blocks[2:4], (blocks[4],))):
        square = jnp.zeros((rows, 1), jnp.float32)
        column = 0
        for part in parts:
            values = part[...].astype(jnp.float32)
            square = square + jnp.sum(values * values, axis=-1, keepdims=True)
            span = slice(column, column + values.shape[1])
            scaled = (values * gain_ref[:, span]).astype(jnp.bfloat16)
            scaled_ref[index * rows : (index + 1) * rows, span] = scaled
            column += values.shape[1]
        squares.append(square)
    scaled = scaled_ref[...]
    gate_proj = lax.dot_general(scaled, gate_ref[...], contract, preferred_element_type=jnp.float32)
    up_proj = lax.dot_general(scaled, up_ref[...], contract, preferred_element_type=jnp.float32)
    square = jnp.concatenate(squares, axis=0)
    out = rest
    if not first:
        gate_proj = gate_proj + rest[0][...]
        up_proj = up_proj + rest[1][...]
        square = square + rest[2][:, :1]
        out = rest[3:]
    if not last:
        out[0][...] = gate_proj
        out[1][...] = up_proj
        out[2][...] = jnp.broadcast_to(square, (4 * rows, 128))
        return
    scale = lax.rsqrt(square / width + EPS)
    gate_proj = gate_proj * scale
    up_proj = up_proj * scale
    active = gate_proj / (1.0 + jnp.exp(-gate_proj)) * up_proj
    for step in range(4):
        place = lax.rem(where_ref[1] + step, 4)
        block = active[step * rows : (step + 1) * rows]
        out[0][:, pl.ds(pl.multiple_of(place * rows, rows), rows)] = block.T.astype(jnp.bfloat16)


def gate_up(where, blocks, gain, gate_part, up_part, earlier, last, width):
    total = 4 * blocks[0].shape[0]
    hidden, depth = gate_part.shape
    vmem = pl.BlockSpec(memory_space=pltpu.VMEM)
    if last:
        out_shape = jax.ShapeDtypeStruct((hidden, total), jnp.bfloat16)
    else:
        out_shape = [
            jax.ShapeDtypeStruct((total, hidden), jnp.float32),
            jax.ShapeDtypeStruct((total, hidden), jnp.float32),
            jax.ShapeDtypeStruct((total, 128), jnp.float32),
        ]
    return pl.pallas_call(
        lambda *refs: gate_up_kernel(earlier is None, last, width, len(blocks), *refs),
        in_specs=[pl.BlockSpec(memory_space=pltpu.SMEM)] + [vmem] * (len(blocks) + 3 + (0 if earlier is None else 3)),
        out_specs=vmem if last else [vmem] * 3,
        out_shape=out_shape,
        scratch_shapes=[pltpu.VMEM((total, depth), jnp.bfloat16)],
        compiler_params=pltpu.CompilerParams(vmem_limit_bytes=SCOPED),
        cost_estimate=pl.CostEstimate(flops=4 * total * depth * hidden, bytes_accessed=4 << 20, transcendentals=total * hidden),
        name="gate_up",
    )(where, *blocks, gain, gate_part, up_part, *(earlier or ()))


def down_kernel(where_ref, own_same, own_other, next_same, next_other, weight_ref, out_ref):
    core, place = where_ref[0], where_ref[1]
    hidden, width = weight_ref.shape[1:]
    z_count, _, rows, _ = out_ref.shape
    for index, (same, other) in enumerate(((own_same, own_other), (next_same, next_other))):
        total = jnp.zeros((z_count * rows, width), jnp.float32)
        for step in range(z_count):
            for values, side in ((same, core), (other, 1 - core)):
                source = lax.rem(place + step, z_count) * 2 + side
                total = total + lax.dot_general(
                    values[step * hidden : (step + 1) * hidden, :],
                    weight_ref[pl.ds(source, 1)][0],
                    (((0,), (0,)), ((), ())),
                    preferred_element_type=jnp.float32,
                )
        side = core if index == 0 else 1 - core
        out_ref[:, pl.ds(side, 1)] = total.astype(jnp.bfloat16).reshape(z_count, 1, rows, width)


def down(where, own_same, own_other, next_same, next_other, weights, z_count):
    width = weights.shape[2]
    rows = own_same.shape[1] // z_count
    vmem = pl.BlockSpec(memory_space=pltpu.VMEM)
    return pl.pallas_call(
        down_kernel,
        in_specs=[pl.BlockSpec(memory_space=pltpu.SMEM)] + [vmem] * 5,
        out_specs=vmem,
        out_shape=jax.ShapeDtypeStruct((z_count, 2, rows, width), jnp.bfloat16),
        compiler_params=pltpu.CompilerParams(vmem_limit_bytes=SCOPED),
        cost_estimate=pl.CostEstimate(flops=4 * 10**9, bytes_accessed=6 << 20, transcendentals=0),
        name="down",
    )(where, own_same, own_other, next_same, next_other, weights)


def combine_kernel(high_ref, low_ref, expert_ref, hidden_ref, out_ref):
    count, _, tile = expert_ref.shape
    for index in range(count):
        rows = expert_ref[index]
        moe = jnp.dot(high_ref[...], rows, preferred_element_type=jnp.float32)
        moe = moe + jnp.dot(low_ref[...], rows, preferred_element_type=jnp.float32)
        span = slice(index * tile, (index + 1) * tile)
        out_ref[:, span] = (hidden_ref[:, span].astype(jnp.float32) + moe).astype(jnp.bfloat16)


def combine(high, low, expert_out, hidden):
    rows, width = hidden.shape
    pieces, slots, tile = expert_out.shape
    whole = pl.BlockSpec((rows, slots), lambda i: (0, 0))
    return pl.pallas_call(
        combine_kernel,
        grid=(pieces // 4,),
        in_specs=[
            whole,
            whole,
            pl.BlockSpec((4, slots, tile), lambda i: (i, 0, 0)),
            pl.BlockSpec((rows, 4 * tile), lambda i: (0, i)),
        ],
        out_specs=pl.BlockSpec((rows, 4 * tile), lambda i: (0, i)),
        out_shape=jax.ShapeDtypeStruct((rows, width), jnp.bfloat16),
        cost_estimate=pl.CostEstimate(flops=4 * rows * slots * width, bytes_accessed=4 << 20, transcendentals=0),
        name="combine",
    )(high, low, expert_out, hidden)


def on_device(
    queries,
    latents,
    latent_gain,
    latent_up,
    document_ids,
    output_weights,
    residual,
    norm_gain,
    expert_ids,
    route_gates,
    gate_weights,
    up_weights,
    down_weights,
):
    seq_count = lax.axis_size("seq")
    group_count = lax.axis_size("exp")
    tok_rows = residual.shape[1]
    model_width = residual.shape[2]
    z_count = seq_count // 2
    place = lax.axis_index("seq")
    core, z_place = place % 2, place // 2
    own = jnp.stack([core, z_place]).astype(jnp.int32)
    swap = [(i, i ^ 1) for i in range(seq_count)]
    around = [(i, (i // 2 + 1 - 2 * (i % 2)) % z_count * 2 + i % 2) for i in range(seq_count)]
    above = [(i, (i + 2) % seq_count) for i in range(seq_count)]
    below = [(i, (i - 2) % seq_count) for i in range(seq_count)]

    normed = rms_scale(latents[0, :, :KV_RANK].astype(jnp.float32), latent_gain).astype(jnp.bfloat16)
    spare = PACKED - KV_RANK - ROPE - 1
    packed = jnp.concatenate(
        [
            normed,
            latents[0, :, KV_RANK:],
            document_ids[0][:, None].astype(jnp.bfloat16),
            jnp.zeros((tok_rows, spare), jnp.bfloat16),
        ],
        axis=1,
    )
    packed, queries = lax.optimization_barrier((packed, queries))
    all_latent = lax.all_gather(packed, "seq", axis=0, tiled=True)
    by_head = split_columns(queries[0], seq_count)
    arrived_queries = lax.all_to_all(by_head, "seq", split_axis=0, concat_axis=0, tiled=True)
    keys, values = keys_and_values(all_latent, latent_up)
    doc_col = all_latent[:, KV_RANK + ROPE : KV_RANK + ROPE + 1]
    doc_row = doc_col.reshape(1, -1)
    head_queries = arrived_queries.reshape(seq_count * tok_rows, -1)

    piece = model_width // seq_count
    down_pieces = split_columns(down_weights[0], seq_count)
    width = model_width // 2
    spans = [slice(0, width), slice(width, model_width)]
    halves = [(gate_weights[0, :, span], up_weights[0, :, span]) for span in spans]
    halves, head_queries = lax.optimization_barrier((halves, head_queries))
    down_pieces, head_queries, keys, values, doc_col, doc_row = lax.optimization_barrier(
        (down_pieces, head_queries, keys, values, doc_col, doc_row)
    )
    down_columns = lax.all_to_all(down_pieces, "seq", split_axis=0, concat_axis=0, tiled=True)

    window = jnp.arange(group_count, dtype=jnp.int32) * GROUP_EXPERTS
    matches = expert_ids[0][:, :, None] == window
    chosen = jnp.any(matches, axis=1).astype(jnp.bfloat16)
    gate_share = jnp.sum(jnp.where(matches, route_gates[0][:, :, None], jnp.zeros((), jnp.float32)), axis=1)
    row_ids = jnp.arange(tok_rows, dtype=jnp.int32)
    earlier = (row_ids[None, :] < row_ids[:, None]).astype(jnp.bfloat16)
    slot_rank = jnp.dot(earlier, chosen, preferred_element_type=jnp.float32)
    slot_ids = jnp.arange(CAP, dtype=jnp.float32)
    slot_picks = chosen.astype(jnp.float32)[:, :, None] * (slot_rank[:, :, None] == slot_ids).astype(jnp.float32)
    slot_picks = slot_picks.reshape(tok_rows, group_count * CAP)
    mixing = slot_picks * jnp.repeat(gate_share, CAP, axis=1)
    picks = slot_picks.astype(jnp.bfloat16)

    high = mixing.astype(jnp.bfloat16)
    low = (mixing - high.astype(jnp.float32)).astype(jnp.bfloat16)
    head_queries, picks, high, low = lax.optimization_barrier((head_queries, picks, high, low))
    head_out = attend(own, head_queries, keys, values, doc_col, doc_row)
    gain = norm_gain[None, :]
    half = head_out.shape[0] // 2

    def across(value):
        return lax.ppermute(value, "seq", swap)

    def up(value):
        return lax.ppermute(value, "seq", above)

    def down_one(value):
        return lax.ppermute(value, "seq", below)

    def turn_round(value):
        return lax.ppermute(value, "seq", around)

    def together(*arrays):
        return lax.optimization_barrier(arrays)

    def project(span):
        product = jnp.dot(head_out, output_weights[:, span], preferred_element_type=jnp.float32).astype(jnp.bfloat16)
        mine, theirs = together(product[:half], product[half:])
        return mine.reshape(z_count, tok_rows, width), theirs.reshape(z_count, tok_rows, width)

    left, right = slice(0, width // 2), slice(width // 2, width)

    def add(arrived, mine, added, step):
        total = arrived.astype(jnp.float32) + mine[(step + 3) % 4].astype(jnp.float32)
        return total + added[step].astype(jnp.float32)

    def dispatch(total, span):
        stage_hidden = (residual[0, :, span].astype(jnp.float32) + total).astype(jnp.bfloat16)
        outgoing = jnp.einsum("ts,td->sd", picks, stage_hidden, preferred_element_type=jnp.float32).astype(jnp.bfloat16)
        arrived = lax.all_to_all(
            outgoing.reshape(group_count, CAP, -1), "exp", split_axis=0, concat_axis=0, tiled=True
        ).reshape(group_count * CAP, -1)
        return stage_hidden, arrived

    mine_a, theirs_a = project(spans[0])
    theirs_a, down_columns = together(theirs_a, down_columns)
    added_a = across(theirs_a)
    run_a = mine_a[0] + added_a[1]
    head_out, run_a = together(head_out, run_a)
    mine_b, theirs_b = project(spans[1])
    run_a = add(turn_round(run_a), mine_a, added_a, 2).astype(jnp.bfloat16)
    theirs_b, run_a = together(theirs_b, run_a)
    added_b = across(theirs_b)
    run_b = mine_b[0] + added_b[1]
    run_a = add(turn_round(run_a), mine_a, added_a, 3).astype(jnp.bfloat16)
    run_b = add(turn_round(run_b), mine_b, added_b, 2).astype(jnp.bfloat16)
    hidden_a, early = dispatch(add(turn_round(run_a), mine_a, added_a, 0), spans[0])
    run_b = add(turn_round(run_b), mine_b, added_b, 3).astype(jnp.bfloat16)
    last_b = turn_round(run_b)
    last_b, early = together(last_b, early)
    hidden_b, late = dispatch(add(last_b, mine_b, added_b, 0), spans[1])
    hidden = [hidden_a, hidden_b]

    carried = [None, None]

    def work(stage, side, rows):
        carried[side] = gate_up(
            own, rows, gain[:, spans[stage]], *halves[stage], carried[side], stage == 1, model_width
        )

    from_above, from_below, late = together(down_one(early), up(early), late)
    far = together(up(from_below[:, left]), down_one(from_above[:, right]))
    early = [early, from_above, *far, from_below]
    early_other = [across(value) for value in early]
    from_above, from_below = together(down_one(late), up(late))
    work(0, 0, early)
    far = [up(from_below[:, left]), down_one(from_above[:, right])]
    far[0], far[1], carried[0] = together(far[0], far[1], carried[0])
    late = [late, from_above, *far, from_below]
    work(0, 1, early_other)
    late[3], carried[1] = together(late[3], carried[1])
    late_other = [across(value) for value in late]
    work(1, 0, late)
    work(1, 1, late_other)

    same = []
    for value in carried:
        middle = value.shape[1] // 2
        from_above, from_below = down_one(value), up(value)
        far = jnp.concatenate([up(from_below[:, :middle]), down_one(from_above[:, middle:])], axis=1)
        same.append(jnp.concatenate([value, from_above, far, from_below], axis=0))
    cross = [across(value) for value in same]
    results = down(own, same[0], cross[1], same[1], cross[0], down_columns, z_count)
    results = results.reshape(seq_count * group_count, CAP, piece)
    returned = lax.all_to_all(results, ("seq", "exp"), split_axis=0, concat_axis=0, tiled=True)
    returned = returned.reshape(seq_count, group_count * CAP, piece)
    return combine(high, low, returned, jnp.concatenate(hidden, axis=1))[None]


def solution(mesh):
    return jax.shard_map(
        on_device,
        mesh=mesh,
        in_specs=(
            P("exp", "seq", None),
            P("exp", "seq", None),
            P(),
            P(None, "seq"),
            P("exp", "seq"),
            P("seq", None),
            P("exp", "seq", None),
            P(),
            P("exp", "seq", None),
            P("exp", "seq", None),
            P("exp", "seq", None),
            P("exp", "seq", None),
            P("exp", "seq", None),
        ),
        out_specs=P("exp", "seq", None),
        check_vma=False,
    )
```

```python
import jax
import jax.numpy as jnp
from jax import lax
from jax.experimental import pallas as pl
from jax.experimental.pallas import tpu as pltpu
from jax.sharding import PartitionSpec as P

NOPE = 128
ROPE = 64
VDIM = 128
KV_RANK = 512
GROUP_EXPERTS = 10
CAP = 8
DOC_MAX = 512
QUERY_BLOCK = 256
PACKED = 640
SCOPED = 24 << 20
LARGE = 58 << 20


EPS = 1e-06
MASKED = -1e30
LOG2_E = 1.4426950408889634


def rms_scale(values, gain):
    mean_sq = jnp.mean(values * values, axis=-1, keepdims=True)
    return values * lax.rsqrt(mean_sq + EPS) * gain


def key_windows(length):
    windows = []
    for start in range(0, length, QUERY_BLOCK):
        first = max(0, start - DOC_MAX + 1) // QUERY_BLOCK * QUERY_BLOCK
        windows.append((start, first, start + QUERY_BLOCK))
    return windows


def split_kernel(in_ref, out_ref):
    pieces, _, share = out_ref.shape
    for index in range(pieces):
        out_ref[index] = in_ref[:, index * share : (index + 1) * share]


def split_columns(array, pieces):
    rows, width = array.shape
    share = width // pieces
    some = pieces // 2
    return pl.pallas_call(
        split_kernel,
        grid=(2,),
        in_specs=[pl.BlockSpec((rows, some * share), lambda i: (0, i))],
        out_specs=pl.BlockSpec((some, rows, share), lambda i: (i, 0, 0)),
        out_shape=jax.ShapeDtypeStruct((pieces, rows, share), array.dtype),
        compiler_params=pltpu.CompilerParams(vmem_limit_bytes=SCOPED),
        cost_estimate=pl.CostEstimate(flops=0, bytes_accessed=4 * rows * width, transcendentals=0),
        name="split_columns",
    )(array)


def shared_kernel(latent_ref, up_ref, key_ref, value_ref):
    key_values = jnp.dot(latent_ref[:, :KV_RANK], up_ref[...], preferred_element_type=jnp.float32)
    tail = latent_ref[:, KV_RANK:].astype(jnp.float32)
    tail = jnp.where(lax.broadcasted_iota(jnp.int32, tail.shape, 1) < ROPE, tail, 0.0)
    wide = NOPE + VDIM
    key_ref[:, :256] = jnp.concatenate([key_values[:, :NOPE], tail], axis=1).astype(jnp.bfloat16)
    second = jnp.concatenate([key_values[:, wide : wide + NOPE], tail], axis=1)
    key_ref[:, 256:] = pltpu.roll(second, ROPE, 1).astype(jnp.bfloat16)
    value_ref[:, :VDIM] = key_values[:, NOPE:wide].astype(jnp.bfloat16)
    value_ref[:, VDIM : 2 * VDIM] = jnp.ones((value_ref.shape[0], VDIM), jnp.bfloat16)
    value_ref[:, 2 * VDIM :] = key_values[:, wide + NOPE :].astype(jnp.bfloat16)


def keys_and_values(latent, up):
    length = latent.shape[0]
    pairs = up.shape[1] // 512
    return pl.pallas_call(
        shared_kernel,
        grid=(pairs,),
        out_shape=[
            jax.ShapeDtypeStruct((length, pairs * 512), jnp.bfloat16),
            jax.ShapeDtypeStruct((length, pairs * 384), jnp.bfloat16),
        ],
        in_specs=[
            pl.BlockSpec((length, PACKED), lambda i: (0, 0)),
            pl.BlockSpec((KV_RANK, 512), lambda i: (0, i)),
        ],
        out_specs=[
            pl.BlockSpec((length, 512), lambda i: (0, i)),
            pl.BlockSpec((length, 384), lambda i: (0, i)),
        ],
        compiler_params=pltpu.CompilerParams(vmem_limit_bytes=LARGE),
        cost_estimate=pl.CostEstimate(flops=2 * length * KV_RANK * 512 * pairs, bytes_accessed=12 << 20, transcendentals=0),
        name="keys_and_values",
    )(latent, up)


def attend_kernel(windows, where_ref, q_ref, key_ref, value_ref, doc_col_ref, doc_row_ref, out_ref, bias_ref):
    @pl.when(pl.program_id(0) == 0)
    def _():
        for index, (start, first, end) in enumerate(windows):
            shape = (QUERY_BLOCK, end - first)
            query_pos = start + lax.broadcasted_iota(jnp.int32, shape, 0)
            key_pos = first + lax.broadcasted_iota(jnp.int32, shape, 1)
            same = doc_col_ref[start : start + QUERY_BLOCK, :] == doc_row_ref[:, first:end]
            bias_ref[index, :, : end - first] = jnp.where((key_pos <= query_pos) & same, 0.0, MASKED)

    scale = (NOPE + ROPE) ** (-0.5) * LOG2_E
    for index, (start, first, end) in enumerate(windows):
        for head in range(2):
            queries = q_ref[start : start + QUERY_BLOCK, head * 128 : head * 128 + 256]
            scores = lax.dot_general(
                queries,
                key_ref[first:end, head * 256 : head * 256 + 256],
                (((1,), (1,)), ((), ())),
                preferred_element_type=jnp.float32,
            )
            scores = scores * scale + bias_ref[index, :, : end - first]
            peak = jnp.max(scores, axis=-1, keepdims=True)
            weights = jnp.exp2(scores - peak).astype(jnp.bfloat16)
            mixed = jnp.dot(
                weights, value_ref[first:end, head * 128 : head * 128 + 256], preferred_element_type=jnp.float32
            )
            low, high = mixed[:, :VDIM], mixed[:, VDIM:]
            result = (low / high if head == 0 else high / low).astype(jnp.bfloat16)
            half = QUERY_BLOCK // 2
            for side in range(2):
                mine = where_ref[0] == side
                turn = 1 - 2 * side
                step = lax.rem((where_ref[1] - index) * turn + 8, 4)
                block = jnp.where(mine, lax.rem(step + 3, 4), 4 + step)
                place = pl.ds(pl.multiple_of(block * half, half), half)
                out_ref[place, head * VDIM : (head + 1) * VDIM] = result[side * half : (side + 1) * half]


def attend(where, head_queries, keys, values, doc_col, doc_row):
    length, width = head_queries.shape
    pairs = width // 384
    windows = key_windows(length)
    widest = max(end - first for _, first, end in windows)
    return pl.pallas_call(
        lambda *refs: attend_kernel(windows, *refs),
        grid_spec=pltpu.PrefetchScalarGridSpec(
            num_scalar_prefetch=1,
            grid=(pairs,),
            in_specs=[
                pl.BlockSpec((length, 384), lambda i, w: (0, i)),
                pl.BlockSpec((length, 512), lambda i, w: (0, i)),
                pl.BlockSpec((length, 384), lambda i, w: (0, i)),
                pl.BlockSpec((length, 1), lambda i, w: (0, 0)),
                pl.BlockSpec((1, length), lambda i, w: (0, 0)),
            ],
            out_specs=pl.BlockSpec((length, 256), lambda i, w: (0, i)),
            scratch_shapes=[pltpu.VMEM((len(windows), QUERY_BLOCK, widest), jnp.float32)],
        ),
        out_shape=jax.ShapeDtypeStruct((length, pairs * 256), jnp.bfloat16),
        compiler_params=pltpu.CompilerParams(vmem_limit_bytes=LARGE),
        cost_estimate=pl.CostEstimate(flops=10**8, bytes_accessed=1 << 20, transcendentals=10**5),
        name="attend",
    )(where, head_queries, keys, values, doc_col, doc_row)


def gate_up_kernel(first, last, width, where_ref, *refs):
    blocks = refs[:5]
    gain_ref, weight_ref = refs[5:7]
    rest = refs[7:]
    scaled_ref = rest[-1]
    squares = []
    rows, depth = blocks[0].shape
    for index, parts in enumerate(((blocks[0],), (blocks[1],), blocks[2:4], (blocks[4],))):
        square = jnp.zeros((rows, 1), jnp.float32)
        column = 0
        for part in parts:
            values = part[...].astype(jnp.float32)
            square = square + jnp.sum(values * values, axis=-1, keepdims=True)
            span = slice(column, column + values.shape[1])
            scaled = (values * gain_ref[:, span]).astype(jnp.bfloat16)
            scaled_ref[index * rows : (index + 1) * rows, span] = scaled
            column += values.shape[1]
        squares.append(square)
    product = lax.dot_general(
        scaled_ref[...], weight_ref[...], (((1,), (1,)), ((), ())), preferred_element_type=jnp.float32
    )
    square = jnp.concatenate(squares, axis=0)
    out = rest
    if not first:
        product = product + rest[0][...]
        square = square + rest[1][:, :1]
        out = rest[2:]
    if not last:
        out[0][...] = product
        out[1][...] = jnp.broadcast_to(square, (4 * rows, 128))
        return
    product = product * lax.rsqrt(square / width + EPS)
    hidden = product.shape[1] // 2
    gate_proj, up_proj = product[:, :hidden], product[:, hidden:]
    active = (gate_proj / (1.0 + jnp.exp(-gate_proj)) * up_proj).astype(jnp.bfloat16)
    for step in range(4):
        place = lax.rem(where_ref[1] + step, 4)
        out[0][pl.ds(pl.multiple_of(place * rows, rows), rows), :] = active[step * rows : (step + 1) * rows]


def gate_up(where, blocks, gain, weights, earlier, last, width):
    total = 4 * blocks[0].shape[0]
    units, depth = weights.shape
    vmem = pl.BlockSpec(memory_space=pltpu.VMEM)
    if last:
        out_shape = jax.ShapeDtypeStruct((total, units // 2), jnp.bfloat16)
    else:
        out_shape = [
            jax.ShapeDtypeStruct((total, units), jnp.float32),
            jax.ShapeDtypeStruct((total, 128), jnp.float32),
        ]
    return pl.pallas_call(
        lambda *refs: gate_up_kernel(earlier is None, last, width, *refs),
        in_specs=[pl.BlockSpec(memory_space=pltpu.SMEM)] + [vmem] * (len(blocks) + 2 + (0 if earlier is None else 2)),
        out_specs=vmem if last else [vmem] * 2,
        out_shape=out_shape,
        scratch_shapes=[pltpu.VMEM((total, depth), jnp.bfloat16)],
        compiler_params=pltpu.CompilerParams(vmem_limit_bytes=SCOPED),
        cost_estimate=pl.CostEstimate(flops=10**6, bytes_accessed=1 << 16, transcendentals=0),
        name="gate_up",
    )(where, *blocks, gain, weights, *(earlier or ()))


def down_kernel(where_ref, active_ref, *refs):
    parts = refs[:8]
    same_ref, other_ref, out_ref, weight_ref, rows_ref = refs[8:]
    z_count, hidden, _ = same_ref.shape
    units = 2 * hidden

    @pl.when(pl.program_id(0) == 0)
    def _():
        for step in range(z_count):
            chip = pl.ds(lax.rem(where_ref[1] + step, z_count), 1)
            weight_ref[step * units : step * units + hidden, :] = same_ref[chip][0]
            weight_ref[step * units + hidden : (step + 1) * units, :] = other_ref[chip][0]

    count = rows_ref.shape[0]
    rows_ref[:, :units] = active_ref[...]
    for index in range(2):

        @pl.when(pl.program_id(0) == index)
        def _(index=index):
            above_ref, left_ref, right_ref, below_ref = parts[4 * index : 4 * index + 4]
            rows_ref[:, units : 2 * units] = above_ref[...]
            rows_ref[: count // 2, 2 * units : 3 * units] = left_ref[...]
            rows_ref[count // 2 :, 2 * units : 3 * units] = right_ref[...]
            rows_ref[:, 3 * units :] = below_ref[...]

    out_ref[...] = jnp.dot(rows_ref[...], weight_ref[...], preferred_element_type=jnp.float32).astype(jnp.bfloat16)


def down(where, active, parts, same, other):
    total, units = active.shape
    z_count, _, width = same.shape
    count = total // 2
    whole = [pl.BlockSpec(value.shape, lambda i, w: (0, 0)) for value in parts]
    weight_spec = pl.BlockSpec(same.shape, lambda i, w: (0, 0, 0))
    return pl.pallas_call(
        down_kernel,
        grid_spec=pltpu.PrefetchScalarGridSpec(
            num_scalar_prefetch=1,
            grid=(2,),
            in_specs=[pl.BlockSpec((count, units), lambda i, w: (i, 0))] + whole + [weight_spec] * 2,
            out_specs=pl.BlockSpec((count, width), lambda i, w: (i, 0)),
            scratch_shapes=[
                pltpu.VMEM((z_count * units, width), jnp.bfloat16),
                pltpu.VMEM((count, z_count * units), jnp.bfloat16),
            ],
        ),
        out_shape=jax.ShapeDtypeStruct((total, width), jnp.bfloat16),
        compiler_params=pltpu.CompilerParams(vmem_limit_bytes=LARGE // 2),
        cost_estimate=pl.CostEstimate(flops=2 * 10**9, bytes_accessed=6 << 20, transcendentals=0),
        name="down",
    )(where, active, *parts, same, other)


def combine_kernel(high_ref, low_ref, expert_ref, hidden_ref, out_ref):
    count, _, tile = expert_ref.shape
    for index in range(count):
        rows = expert_ref[index]
        moe = jnp.dot(high_ref[...], rows, preferred_element_type=jnp.float32)
        moe = moe + jnp.dot(low_ref[...], rows, preferred_element_type=jnp.float32)
        span = slice(index * tile, (index + 1) * tile)
        out_ref[:, span] = (hidden_ref[:, span].astype(jnp.float32) + moe).astype(jnp.bfloat16)


def combine(high, low, expert_out, hidden):
    rows, width = hidden.shape
    pieces, slots, tile = expert_out.shape
    whole = pl.BlockSpec((rows, slots), lambda i: (0, 0))
    return pl.pallas_call(
        combine_kernel,
        grid=(pieces // 2,),
        in_specs=[
            whole,
            whole,
            pl.BlockSpec((2, slots, tile), lambda i: (i, 0, 0)),
            pl.BlockSpec((rows, 2 * tile), lambda i: (0, i)),
        ],
        out_specs=pl.BlockSpec((rows, 2 * tile), lambda i: (0, i)),
        out_shape=jax.ShapeDtypeStruct((rows, width), jnp.bfloat16),
        cost_estimate=pl.CostEstimate(flops=4 * rows * slots * width, bytes_accessed=4 << 20, transcendentals=0),
        name="combine",
    )(high, low, expert_out, hidden)


def on_device(
    queries,
    latents,
    latent_gain,
    latent_up,
    document_ids,
    output_weights,
    residual,
    norm_gain,
    expert_ids,
    route_gates,
    gate_weights,
    up_weights,
    down_weights,
):
    seq = ("z", "core")
    seq_count = lax.axis_size(seq)
    group_count = lax.axis_size("exp")
    tok_rows = residual.shape[1]
    model_width = residual.shape[2]
    z_count = lax.axis_size("z")
    core, z_place = lax.axis_index("core"), lax.axis_index("z")
    own = jnp.stack([core, z_place]).astype(jnp.int32)
    around = [(i, (i // 2 + 1 - 2 * (i % 2)) % z_count * 2 + i % 2) for i in range(seq_count)]
    reverse = [(i, (i // 2 - 1 + 2 * (i % 2)) % z_count * 2 + i % 2) for i in range(seq_count)]
    above = [(i, (i + 1) % z_count) for i in range(z_count)]
    below = [(i, (i - 1) % z_count) for i in range(z_count)]

    normed = rms_scale(latents[0, :, :KV_RANK].astype(jnp.float32), latent_gain).astype(jnp.bfloat16)
    spare = PACKED - KV_RANK - ROPE - 1
    packed = jnp.concatenate(
        [
            normed,
            latents[0, :, KV_RANK:],
            document_ids[0][:, None].astype(jnp.bfloat16),
            jnp.zeros((tok_rows, spare), jnp.bfloat16),
        ],
        axis=1,
    )
    packed, queries = lax.optimization_barrier((packed, queries))
    all_latent = lax.all_gather(packed, seq, axis=0, tiled=True)
    by_head = split_columns(queries[0], seq_count)
    arrived_queries = lax.all_to_all(by_head, seq, split_axis=0, concat_axis=0, tiled=True)
    keys, values = keys_and_values(all_latent, latent_up)
    doc_col = all_latent[:, KV_RANK + ROPE : KV_RANK + ROPE + 1]
    doc_row = doc_col.reshape(1, -1)
    head_queries = arrived_queries.reshape(seq_count * tok_rows, -1)

    piece = model_width // z_count
    down_pieces = split_columns(down_weights[0], z_count)
    width = model_width // 2
    spans = [slice(0, width), slice(width, model_width)]
    def across(value):
        return lax.ppermute(value, "core", [(0, 1), (1, 0)])

    others = across(gate_weights[0]), across(up_weights[0])
    halves = []
    for span in spans:
        units = [gate_weights[0, :, span], others[0][:, span], up_weights[0, :, span], others[1][:, span]]
        halves.append(jnp.concatenate(units, axis=0))
    halves, head_queries = lax.optimization_barrier((halves, head_queries))
    down_pieces, keys = lax.optimization_barrier((down_pieces, keys))
    head_queries, keys, values, doc_col, doc_row = lax.optimization_barrier(
        (head_queries, keys, values, doc_col, doc_row)
    )
    down_columns = lax.all_to_all(down_pieces, "z", split_axis=0, concat_axis=0, tiled=True)

    window = jnp.arange(group_count, dtype=jnp.int32) * GROUP_EXPERTS
    matches = expert_ids[0][:, :, None] == window
    chosen = jnp.any(matches, axis=1).astype(jnp.bfloat16)
    gate_share = jnp.sum(jnp.where(matches, route_gates[0][:, :, None], jnp.zeros((), jnp.float32)), axis=1)
    row_ids = jnp.arange(tok_rows, dtype=jnp.int32)
    earlier = (row_ids[None, :] < row_ids[:, None]).astype(jnp.bfloat16)
    slot_rank = jnp.dot(earlier, chosen, preferred_element_type=jnp.float32)
    slot_ids = jnp.arange(CAP, dtype=jnp.float32)
    slot_picks = chosen.astype(jnp.float32)[:, :, None] * (slot_rank[:, :, None] == slot_ids).astype(jnp.float32)
    slot_picks = slot_picks.reshape(tok_rows, group_count * CAP)
    mixing = slot_picks * jnp.repeat(gate_share, CAP, axis=1)
    picks = slot_picks.astype(jnp.bfloat16)

    high = mixing.astype(jnp.bfloat16)
    low = (mixing - high.astype(jnp.float32)).astype(jnp.bfloat16)
    head_queries, picks, high, low = lax.optimization_barrier((head_queries, picks, high, low))
    head_out = attend(own, head_queries, keys, values, doc_col, doc_row)
    gain = norm_gain[None, :]
    half = head_out.shape[0] // 2

    def up(value):
        return lax.ppermute(value, "z", above)

    def down_one(value):
        return lax.ppermute(value, "z", below)

    def turn_round(value):
        return lax.ppermute(value, seq, around)

    def turn_back(value):
        return lax.ppermute(value, seq, reverse)

    def together(*arrays):
        return lax.optimization_barrier(arrays)

    def project(span):
        product = jnp.dot(head_out, output_weights[:, span], preferred_element_type=jnp.float32).astype(jnp.bfloat16)
        mine, theirs = together(product[:half], product[half:])
        return mine.reshape(z_count, tok_rows, width), theirs.reshape(z_count, tok_rows, width)

    left, right = slice(0, width // 2), slice(width // 2, width)

    def add(arrived, mine, added, step):
        total = arrived.astype(jnp.float32) + mine[(step + 3) % 4].astype(jnp.float32)
        return total + added[step].astype(jnp.float32)

    def dispatch(total, span):
        stage_hidden = (residual[0, :, span].astype(jnp.float32) + total).astype(jnp.bfloat16)
        outgoing = jnp.einsum("ts,td->sd", picks, stage_hidden, preferred_element_type=jnp.float32).astype(jnp.bfloat16)
        arrived = lax.all_to_all(
            outgoing.reshape(group_count, CAP, -1), "exp", split_axis=0, concat_axis=0, tiled=True
        ).reshape(group_count * CAP, -1)
        return stage_hidden, arrived

    mine_a, theirs_a = project(spans[0])
    theirs_a, down_columns = together(theirs_a, down_columns)
    added_a = across(theirs_a)
    run_a = mine_a[0] + added_a[1]
    head_out, run_a = together(head_out, run_a)
    mine_b, theirs_b = project(spans[1])
    run_a = add(turn_round(run_a), mine_a, added_a, 2).astype(jnp.bfloat16)
    theirs_b, run_a = together(theirs_b, run_a)
    added_b = across(theirs_b)
    run_b = mine_b[2] + added_b[3]
    run_a = add(turn_round(run_a), mine_a, added_a, 3).astype(jnp.bfloat16)
    run_b = add(turn_back(run_b), mine_b, added_b, 2).astype(jnp.bfloat16)
    hidden_a, early = dispatch(add(turn_round(run_a), mine_a, added_a, 0), spans[0])
    run_b = add(turn_back(run_b), mine_b, added_b, 1).astype(jnp.bfloat16)
    last_b = turn_back(run_b)
    down_other = across(down_columns)
    last_b, early, down_other = together(last_b, early, down_other)
    hidden_b, late = dispatch(add(last_b, mine_b, added_b, 0), spans[1])
    hidden = [hidden_a, hidden_b]

    def gather(value, cut, more):
        from_above, from_below, *more = together(down_one(value), up(value), *more)
        return [from_above, up(from_below[cut[0]]), down_one(from_above[cut[1]]), from_below], more

    columns = (slice(None), left), (slice(None), right)
    blocks, (late,) = gather(early, columns, [late])
    carried = gate_up(own, [early] + blocks, gain[:, spans[0]], halves[0], None, False, model_width)
    blocks, _ = gather(late, columns, [])
    blocks[1], blocks[2], *carried = together(blocks[1], blocks[2], *carried)
    active = gate_up(own, [late] + blocks, gain[:, spans[1]], halves[1], carried, True, model_width)
    middle = active.shape[0] // 2
    quarter = middle // 2
    parts = []
    for rows in (slice(0, middle), slice(middle, None)):
        parts += gather(active[rows], (slice(0, quarter), slice(quarter, None)), [])[0]
    results = down(own, active, parts, down_columns, down_other)
    results = results.reshape(z_count * group_count, CAP, piece)
    returned = lax.all_to_all(results, ("z", "exp"), split_axis=0, concat_axis=0, tiled=True)
    returned = returned.reshape(z_count, group_count * CAP, piece)
    return combine(high, low, returned, jnp.concatenate(hidden, axis=1))[None]


def solution(mesh):
    mesh = jax.sharding.Mesh(mesh.devices.reshape(-1, 2, mesh.shape["exp"]), ("z", "core", "exp"))
    return jax.shard_map(
        on_device,
        mesh=mesh,
        in_specs=(
            P("exp", ("z", "core"), None),
            P("exp", ("z", "core"), None),
            P(),
            P(None, ("z", "core")),
            P("exp", ("z", "core")),
            P(("z", "core"), None),
            P("exp", ("z", "core"), None),
            P(),
            P("exp", ("z", "core"), None),
            P("exp", ("z", "core"), None),
            P("exp", ("z", "core"), None),
            P("exp", ("z", "core"), None),
            P("exp", ("z", "core"), None),
        ),
        out_specs=P("exp", ("z", "core"), None),
        check_vma=False,
    )
```

```python
import jax
import jax.numpy as jnp
from jax import lax
from jax.experimental import pallas as pl
from jax.experimental.pallas import tpu as pltpu
from jax.sharding import PartitionSpec as P

NOPE = 128
ROPE = 64
VDIM = 128
KV_RANK = 512
GROUP_EXPERTS = 10
CAP = 8
DOC_MAX = 512
QUERY_BLOCK = 256
PACKED = 640
SCOPED = 24 << 20
LARGE = 58 << 20


EPS = 1e-06
MASKED = -1e30
LOG2_E = 1.4426950408889634


def rms_scale(values, gain):
    mean_sq = jnp.mean(values * values, axis=-1, keepdims=True)
    return values * lax.rsqrt(mean_sq + EPS) * gain


def key_windows(length):
    windows = []
    for start in range(0, length, QUERY_BLOCK):
        first = max(0, start - DOC_MAX + 1) // QUERY_BLOCK * QUERY_BLOCK
        windows.append((start, first, start + QUERY_BLOCK))
    return windows


def split_kernel(in_ref, out_ref):
    pieces, _, share = out_ref.shape
    for index in range(pieces):
        out_ref[index] = in_ref[:, index * share : (index + 1) * share]


def split_columns(array, pieces):
    rows, width = array.shape
    share = width // pieces
    some = pieces // 2
    return pl.pallas_call(
        split_kernel,
        grid=(2,),
        in_specs=[pl.BlockSpec((rows, some * share), lambda i: (0, i))],
        out_specs=pl.BlockSpec((some, rows, share), lambda i: (i, 0, 0)),
        out_shape=jax.ShapeDtypeStruct((pieces, rows, share), array.dtype),
        compiler_params=pltpu.CompilerParams(vmem_limit_bytes=SCOPED),
        cost_estimate=pl.CostEstimate(flops=0, bytes_accessed=4 * rows * width, transcendentals=0),
        name="split_columns",
    )(array)


def shared_kernel(latent_ref, up_ref, key_ref, value_ref):
    key_values = jnp.dot(latent_ref[:, :KV_RANK], up_ref[...], preferred_element_type=jnp.float32)
    tail = latent_ref[:, KV_RANK:].astype(jnp.float32)
    tail = jnp.where(lax.broadcasted_iota(jnp.int32, tail.shape, 1) < ROPE, tail, 0.0)
    wide = NOPE + VDIM
    key_ref[:, :256] = jnp.concatenate([key_values[:, :NOPE], tail], axis=1).astype(jnp.bfloat16)
    second = jnp.concatenate([key_values[:, wide : wide + NOPE], tail], axis=1)
    key_ref[:, 256:] = pltpu.roll(second, ROPE, 1).astype(jnp.bfloat16)
    value_ref[:, :VDIM] = key_values[:, NOPE:wide].astype(jnp.bfloat16)
    value_ref[:, VDIM : 2 * VDIM] = jnp.ones((value_ref.shape[0], VDIM), jnp.bfloat16)
    value_ref[:, 2 * VDIM :] = key_values[:, wide + NOPE :].astype(jnp.bfloat16)


def keys_and_values(latent, up):
    length = latent.shape[0]
    pairs = up.shape[1] // 512
    return pl.pallas_call(
        shared_kernel,
        grid=(pairs,),
        out_shape=[
            jax.ShapeDtypeStruct((length, pairs * 512), jnp.bfloat16),
            jax.ShapeDtypeStruct((length, pairs * 384), jnp.bfloat16),
        ],
        in_specs=[
            pl.BlockSpec((length, PACKED), lambda i: (0, 0)),
            pl.BlockSpec((KV_RANK, 512), lambda i: (0, i)),
        ],
        out_specs=[
            pl.BlockSpec((length, 512), lambda i: (0, i)),
            pl.BlockSpec((length, 384), lambda i: (0, i)),
        ],
        compiler_params=pltpu.CompilerParams(vmem_limit_bytes=LARGE),
        cost_estimate=pl.CostEstimate(flops=2 * length * KV_RANK * 512 * pairs, bytes_accessed=12 << 20, transcendentals=0),
        name="keys_and_values",
    )(latent, up)


def attend_kernel(windows, where_ref, q_ref, key_ref, value_ref, doc_col_ref, doc_row_ref, out_ref, bias_ref):
    @pl.when(pl.program_id(0) == 0)
    def _():
        for index, (start, first, end) in enumerate(windows):
            shape = (QUERY_BLOCK, end - first)
            query_pos = start + lax.broadcasted_iota(jnp.int32, shape, 0)
            key_pos = first + lax.broadcasted_iota(jnp.int32, shape, 1)
            same = doc_col_ref[start : start + QUERY_BLOCK, :] == doc_row_ref[:, first:end]
            bias_ref[index, :, : end - first] = jnp.where((key_pos <= query_pos) & same, 0.0, MASKED)

    scale = (NOPE + ROPE) ** (-0.5) * LOG2_E
    for index, (start, first, end) in enumerate(windows):
        for head in range(2):
            queries = q_ref[start : start + QUERY_BLOCK, head * 128 : head * 128 + 256]
            scores = lax.dot_general(
                queries,
                key_ref[first:end, head * 256 : head * 256 + 256],
                (((1,), (1,)), ((), ())),
                preferred_element_type=jnp.float32,
            )
            scores = scores * scale + bias_ref[index, :, : end - first]
            peak = jnp.max(scores, axis=-1, keepdims=True)
            weights = jnp.exp2(scores - peak).astype(jnp.bfloat16)
            mixed = jnp.dot(
                weights, value_ref[first:end, head * 128 : head * 128 + 256], preferred_element_type=jnp.float32
            )
            low, high = mixed[:, :VDIM], mixed[:, VDIM:]
            result = (low / high if head == 0 else high / low).astype(jnp.bfloat16)
            half = QUERY_BLOCK // 2
            for side in range(2):
                mine = where_ref[0] == side
                turn = 1 - 2 * side
                step = lax.rem((where_ref[1] - index) * turn + 8, 4)
                block = jnp.where(mine, lax.rem(step + 3, 4), 4 + step)
                place = pl.ds(pl.multiple_of(block * half, half), half)
                out_ref[place, head * VDIM : (head + 1) * VDIM] = result[side * half : (side + 1) * half]


def attend(where, head_queries, keys, values, doc_col, doc_row):
    length, width = head_queries.shape
    pairs = width // 384
    windows = key_windows(length)
    widest = max(end - first for _, first, end in windows)
    return pl.pallas_call(
        lambda *refs: attend_kernel(windows, *refs),
        grid_spec=pltpu.PrefetchScalarGridSpec(
            num_scalar_prefetch=1,
            grid=(pairs,),
            in_specs=[
                pl.BlockSpec((length, 384), lambda i, w: (0, i)),
                pl.BlockSpec((length, 512), lambda i, w: (0, i)),
                pl.BlockSpec((length, 384), lambda i, w: (0, i)),
                pl.BlockSpec((length, 1), lambda i, w: (0, 0)),
                pl.BlockSpec((1, length), lambda i, w: (0, 0)),
            ],
            out_specs=pl.BlockSpec((length, 256), lambda i, w: (0, i)),
            scratch_shapes=[pltpu.VMEM((len(windows), QUERY_BLOCK, widest), jnp.float32)],
        ),
        out_shape=jax.ShapeDtypeStruct((length, pairs * 256), jnp.bfloat16),
        compiler_params=pltpu.CompilerParams(vmem_limit_bytes=LARGE),
        cost_estimate=pl.CostEstimate(flops=10**8, bytes_accessed=1 << 20, transcendentals=10**5),
        name="attend",
    )(where, head_queries, keys, values, doc_col, doc_row)


def gate_up_kernel(first, last, width, where_ref, *refs):
    blocks = refs[:5]
    gain_ref, weight_ref = refs[5:7]
    rest = refs[7:]
    scaled_ref = rest[-1]
    squares = []
    rows, depth = blocks[0].shape
    for index, parts in enumerate(((blocks[0],), (blocks[1],), blocks[2:4], (blocks[4],))):
        square = jnp.zeros((rows, 1), jnp.float32)
        column = 0
        for part in parts:
            values = part[...].astype(jnp.float32)
            square = square + jnp.sum(values * values, axis=-1, keepdims=True)
            span = slice(column, column + values.shape[1])
            scaled = (values * gain_ref[:, span]).astype(jnp.bfloat16)
            scaled_ref[index * rows : (index + 1) * rows, span] = scaled
            column += values.shape[1]
        squares.append(square)
    product = lax.dot_general(
        scaled_ref[...], weight_ref[...], (((1,), (1,)), ((), ())), preferred_element_type=jnp.float32
    )
    square = jnp.concatenate(squares, axis=0)
    out = rest
    if not first:
        product = product + rest[0][...]
        square = square + rest[1][:, :1]
        out = rest[2:]
    if not last:
        out[0][...] = product
        out[1][...] = jnp.broadcast_to(square, (4 * rows, 128))
        return
    product = product * lax.rsqrt(square / width + EPS)
    hidden = product.shape[1] // 2
    gate_proj, up_proj = product[:, :hidden], product[:, hidden:]
    active = (gate_proj / (1.0 + jnp.exp(-gate_proj)) * up_proj).astype(jnp.bfloat16)
    for step in range(4):
        place = lax.rem(where_ref[1] + step, 4)
        out[0][pl.ds(pl.multiple_of(place * rows, rows), rows), :] = active[step * rows : (step + 1) * rows]


def gate_up(where, blocks, gain, weights, earlier, last, width):
    total = 4 * blocks[0].shape[0]
    units, depth = weights.shape
    vmem = pl.BlockSpec(memory_space=pltpu.VMEM)
    if last:
        out_shape = jax.ShapeDtypeStruct((total, units // 2), jnp.bfloat16)
    else:
        out_shape = [
            jax.ShapeDtypeStruct((total, units), jnp.float32),
            jax.ShapeDtypeStruct((total, 128), jnp.float32),
        ]
    return pl.pallas_call(
        lambda *refs: gate_up_kernel(earlier is None, last, width, *refs),
        in_specs=[pl.BlockSpec(memory_space=pltpu.SMEM)] + [vmem] * (len(blocks) + 2 + (0 if earlier is None else 2)),
        out_specs=vmem if last else [vmem] * 2,
        out_shape=out_shape,
        scratch_shapes=[pltpu.VMEM((total, depth), jnp.bfloat16)],
        compiler_params=pltpu.CompilerParams(vmem_limit_bytes=SCOPED),
        cost_estimate=pl.CostEstimate(flops=10**6, bytes_accessed=1 << 16, transcendentals=0),
        name="gate_up",
    )(where, *blocks, gain, weights, *(earlier or ()))


def down_kernel(where_ref, active_ref, *refs):
    parts = refs[:8]
    same_ref, other_ref, out_ref, weight_ref, rows_ref = refs[8:]
    z_count, hidden, _ = same_ref.shape
    units = 2 * hidden

    @pl.when(pl.program_id(0) == 0)
    def _():
        for step in range(z_count):
            chip = pl.ds(lax.rem(where_ref[1] + step, z_count), 1)
            weight_ref[step * units : step * units + hidden, :] = same_ref[chip][0]
            weight_ref[step * units + hidden : (step + 1) * units, :] = other_ref[chip][0]

    count = rows_ref.shape[0]
    rows_ref[:, :units] = active_ref[...]
    for index in range(2):

        @pl.when(pl.program_id(0) == index)
        def _(index=index):
            above_ref, left_ref, right_ref, below_ref = parts[4 * index : 4 * index + 4]
            rows_ref[:, units : 2 * units] = above_ref[...]
            rows_ref[: count // 2, 2 * units : 3 * units] = left_ref[...]
            rows_ref[count // 2 :, 2 * units : 3 * units] = right_ref[...]
            rows_ref[:, 3 * units :] = below_ref[...]

    out_ref[...] = jnp.dot(rows_ref[...], weight_ref[...], preferred_element_type=jnp.float32).astype(jnp.bfloat16)


def down(where, active, parts, same, other):
    total, units = active.shape
    z_count, _, width = same.shape
    count = total // 2
    whole = [pl.BlockSpec(value.shape, lambda i, w: (0, 0)) for value in parts]
    weight_spec = pl.BlockSpec(same.shape, lambda i, w: (0, 0, 0))
    return pl.pallas_call(
        down_kernel,
        grid_spec=pltpu.PrefetchScalarGridSpec(
            num_scalar_prefetch=1,
            grid=(2,),
            in_specs=[pl.BlockSpec((count, units), lambda i, w: (i, 0))] + whole + [weight_spec] * 2,
            out_specs=pl.BlockSpec((count, width), lambda i, w: (i, 0)),
            scratch_shapes=[
                pltpu.VMEM((z_count * units, width), jnp.bfloat16),
                pltpu.VMEM((count, z_count * units), jnp.bfloat16),
            ],
        ),
        out_shape=jax.ShapeDtypeStruct((total, width), jnp.bfloat16),
        compiler_params=pltpu.CompilerParams(vmem_limit_bytes=LARGE // 2),
        cost_estimate=pl.CostEstimate(flops=2 * 10**9, bytes_accessed=6 << 20, transcendentals=0),
        name="down",
    )(where, active, *parts, same, other)


def combine_kernel(high_ref, low_ref, expert_ref, hidden_ref, out_ref):
    count, _, tile = expert_ref.shape
    for index in range(count):
        rows = expert_ref[index]
        moe = jnp.dot(high_ref[...], rows, preferred_element_type=jnp.float32)
        moe = moe + jnp.dot(low_ref[...], rows, preferred_element_type=jnp.float32)
        span = slice(index * tile, (index + 1) * tile)
        out_ref[:, span] = (hidden_ref[:, span].astype(jnp.float32) + moe).astype(jnp.bfloat16)


def combine(high, low, expert_out, hidden):
    rows, width = hidden.shape
    pieces, slots, tile = expert_out.shape
    whole = pl.BlockSpec((rows, slots), lambda i: (0, 0))
    return pl.pallas_call(
        combine_kernel,
        grid=(pieces // 2,),
        in_specs=[
            whole,
            whole,
            pl.BlockSpec((2, slots, tile), lambda i: (i, 0, 0)),
            pl.BlockSpec((rows, 2 * tile), lambda i: (0, i)),
        ],
        out_specs=pl.BlockSpec((rows, 2 * tile), lambda i: (0, i)),
        out_shape=jax.ShapeDtypeStruct((rows, width), jnp.bfloat16),
        cost_estimate=pl.CostEstimate(flops=4 * rows * slots * width, bytes_accessed=4 << 20, transcendentals=0),
        name="combine",
    )(high, low, expert_out, hidden)


def on_device(
    queries,
    latents,
    latent_gain,
    latent_up,
    document_ids,
    output_weights,
    residual,
    norm_gain,
    expert_ids,
    route_gates,
    gate_weights,
    up_weights,
    down_weights,
):
    seq = ("z", "core")
    seq_count = lax.axis_size(seq)
    group_count = lax.axis_size("exp")
    tok_rows = residual.shape[1]
    model_width = residual.shape[2]
    z_count = lax.axis_size("z")
    core, z_place = lax.axis_index("core"), lax.axis_index("z")
    own = jnp.stack([core, z_place]).astype(jnp.int32)
    around = [(i, (i // 2 + 1 - 2 * (i % 2)) % z_count * 2 + i % 2) for i in range(seq_count)]
    reverse = [(i, (i // 2 - 1 + 2 * (i % 2)) % z_count * 2 + i % 2) for i in range(seq_count)]
    above = [(i, (i + 1) % z_count) for i in range(z_count)]
    below = [(i, (i - 1) % z_count) for i in range(z_count)]

    normed = rms_scale(latents[0, :, :KV_RANK].astype(jnp.float32), latent_gain).astype(jnp.bfloat16)
    spare = PACKED - KV_RANK - ROPE - 1
    packed = jnp.concatenate(
        [
            normed,
            latents[0, :, KV_RANK:],
            document_ids[0][:, None].astype(jnp.bfloat16),
            jnp.zeros((tok_rows, spare), jnp.bfloat16),
        ],
        axis=1,
    )
    packed, queries = lax.optimization_barrier((packed, queries))
    all_latent = lax.all_gather(packed, seq, axis=0, tiled=True)
    by_head = split_columns(queries[0], seq_count)
    arrived_queries = lax.all_to_all(by_head, seq, split_axis=0, concat_axis=0, tiled=True)
    keys, values = keys_and_values(all_latent, latent_up)
    doc_col = all_latent[:, KV_RANK + ROPE : KV_RANK + ROPE + 1]
    doc_row = doc_col.reshape(1, -1)
    head_queries = arrived_queries.reshape(seq_count * tok_rows, -1)

    piece = model_width // z_count
    down_pieces = split_columns(down_weights[0], z_count)
    width = model_width // 2
    spans = [slice(0, width), slice(width, model_width)]
    def across(value):
        return lax.ppermute(value, "core", [(0, 1), (1, 0)])

    others = across(gate_weights[0]), across(up_weights[0])
    halves = []
    for span in spans:
        units = [gate_weights[0, :, span], others[0][:, span], up_weights[0, :, span], others[1][:, span]]
        halves.append(jnp.concatenate(units, axis=0))
    halves, head_queries = lax.optimization_barrier((halves, head_queries))
    down_pieces, keys = lax.optimization_barrier((down_pieces, keys))
    head_queries, keys, values, doc_col, doc_row = lax.optimization_barrier(
        (head_queries, keys, values, doc_col, doc_row)
    )
    down_columns = lax.all_to_all(down_pieces, "z", split_axis=0, concat_axis=0, tiled=True)

    window = jnp.arange(group_count, dtype=jnp.int32) * GROUP_EXPERTS
    matches = expert_ids[0][:, :, None] == window
    chosen = jnp.any(matches, axis=1).astype(jnp.bfloat16)
    gate_share = jnp.sum(jnp.where(matches, route_gates[0][:, :, None], jnp.zeros((), jnp.float32)), axis=1)
    row_ids = jnp.arange(tok_rows, dtype=jnp.int32)
    earlier = (row_ids[None, :] < row_ids[:, None]).astype(jnp.bfloat16)
    slot_rank = jnp.dot(earlier, chosen, preferred_element_type=jnp.float32)
    slot_ids = jnp.arange(CAP, dtype=jnp.float32)
    slot_picks = chosen.astype(jnp.float32)[:, :, None] * (slot_rank[:, :, None] == slot_ids).astype(jnp.float32)
    slot_picks = slot_picks.reshape(tok_rows, group_count * CAP)
    mixing = slot_picks * jnp.repeat(gate_share, CAP, axis=1)
    picks = slot_picks.astype(jnp.bfloat16)

    high = mixing.astype(jnp.bfloat16)
    low = (mixing - high.astype(jnp.float32)).astype(jnp.bfloat16)
    head_queries, picks, high, low = lax.optimization_barrier((head_queries, picks, high, low))
    head_out = attend(own, head_queries, keys, values, doc_col, doc_row)
    gain = norm_gain[None, :]
    half = head_out.shape[0] // 2

    def up(value):
        return lax.ppermute(value, "z", above)

    def down_one(value):
        return lax.ppermute(value, "z", below)

    def turn_round(value):
        return lax.ppermute(value, seq, around)

    def turn_back(value):
        return lax.ppermute(value, seq, reverse)

    def together(*arrays):
        return lax.optimization_barrier(arrays)

    def project(span):
        product = jnp.dot(head_out, output_weights[:, span], preferred_element_type=jnp.float32).astype(jnp.bfloat16)
        mine, theirs = together(product[:half], product[half:])
        return mine.reshape(z_count, tok_rows, width), theirs.reshape(z_count, tok_rows, width)

    left, right = slice(0, width // 2), slice(width // 2, width)

    def add(arrived, mine, added, step):
        total = arrived.astype(jnp.float32) + mine[(step + 3) % 4].astype(jnp.float32)
        return total + added[step].astype(jnp.float32)

    def dispatch(total, span):
        stage_hidden = (residual[0, :, span].astype(jnp.float32) + total).astype(jnp.bfloat16)
        outgoing = jnp.einsum("ts,td->sd", picks, stage_hidden, preferred_element_type=jnp.float32).astype(jnp.bfloat16)
        arrived = lax.all_to_all(
            outgoing.reshape(group_count, CAP, -1), "exp", split_axis=0, concat_axis=0, tiled=True
        ).reshape(group_count * CAP, -1)
        return stage_hidden, arrived

    mine_a, theirs_a = project(spans[0])
    theirs_a, down_columns = together(theirs_a, down_columns)
    added_a = across(theirs_a)
    run_a = mine_a[0] + added_a[1]
    head_out, run_a = together(head_out, run_a)
    mine_b, theirs_b = project(spans[1])
    run_a = add(turn_round(run_a), mine_a, added_a, 2).astype(jnp.bfloat16)
    theirs_b, run_a = together(theirs_b, run_a)
    added_b = across(theirs_b)
    run_b = mine_b[2] + added_b[3]
    run_b, down_columns = together(run_b, down_columns)
    down_other = across(down_columns)
    run_a = add(turn_round(run_a), mine_a, added_a, 3).astype(jnp.bfloat16)
    run_b = add(turn_back(run_b), mine_b, added_b, 2).astype(jnp.bfloat16)
    hidden_a, early = dispatch(add(turn_round(run_a), mine_a, added_a, 0), spans[0])
    run_b = add(turn_back(run_b), mine_b, added_b, 1).astype(jnp.bfloat16)
    last_b = turn_back(run_b)
    last_b, early, down_other = together(last_b, early, down_other)
    hidden_b, late = dispatch(add(last_b, mine_b, added_b, 0), spans[1])
    hidden = [hidden_a, hidden_b]

    def gather(value, cut, more):
        from_above, from_below, *more = together(down_one(value), up(value), *more)
        return [from_above, up(from_below[cut[0]]), down_one(from_above[cut[1]]), from_below], more

    columns = (slice(None), left), (slice(None), right)
    blocks, (late,) = gather(early, columns, [late])
    carried = gate_up(own, [early] + blocks, gain[:, spans[0]], halves[0], None, False, model_width)
    blocks, _ = gather(late, columns, [])
    blocks[1], blocks[2], *carried = together(blocks[1], blocks[2], *carried)
    active = gate_up(own, [late] + blocks, gain[:, spans[1]], halves[1], carried, True, model_width)
    middle = active.shape[0] // 2
    quarter = middle // 2
    parts = []
    for rows in (slice(0, middle), slice(middle, None)):
        parts += gather(active[rows], (slice(0, quarter), slice(quarter, None)), [])[0]
    results = down(own, active, parts, down_columns, down_other)
    results = results.reshape(z_count * group_count, CAP, piece)
    returned = lax.all_to_all(results, ("z", "exp"), split_axis=0, concat_axis=0, tiled=True)
    returned = returned.reshape(z_count, group_count * CAP, piece)
    return combine(high, low, returned, jnp.concatenate(hidden, axis=1))[None]


def solution(mesh):
    mesh = jax.sharding.Mesh(mesh.devices.reshape(-1, 2, mesh.shape["exp"]), ("z", "core", "exp"))
    return jax.shard_map(
        on_device,
        mesh=mesh,
        in_specs=(
            P("exp", ("z", "core"), None),
            P("exp", ("z", "core"), None),
            P(),
            P(None, ("z", "core")),
            P("exp", ("z", "core")),
            P(("z", "core"), None),
            P("exp", ("z", "core"), None),
            P(),
            P("exp", ("z", "core"), None),
            P("exp", ("z", "core"), None),
            P("exp", ("z", "core"), None),
            P("exp", ("z", "core"), None),
            P("exp", ("z", "core"), None),
        ),
        out_specs=P("exp", ("z", "core"), None),
        check_vma=False,
    )
```

```python
import jax
import jax.numpy as jnp
from jax import lax
from jax.experimental import pallas as pl
from jax.experimental.pallas import tpu as pltpu
from jax.sharding import PartitionSpec as P

NOPE = 128
ROPE = 64
VDIM = 128
KV_RANK = 512
GROUP_EXPERTS = 10
CAP = 8
DOC_MAX = 512
QUERY_BLOCK = 256
PACKED = 640
SCOPED = 24 << 20
LARGE = 58 << 20


EPS = 1e-06
MASKED = -1e30
LOG2_E = 1.4426950408889634


def rms_scale(values, gain):
    mean_sq = jnp.mean(values * values, axis=-1, keepdims=True)
    return values * lax.rsqrt(mean_sq + EPS) * gain


def key_windows(length):
    windows = []
    for start in range(0, length, QUERY_BLOCK):
        first = max(0, start - DOC_MAX + 1) // QUERY_BLOCK * QUERY_BLOCK
        windows.append((start, first, start + QUERY_BLOCK))
    return windows


def split_kernel(in_ref, out_ref):
    pieces, _, share = out_ref.shape
    for index in range(pieces):
        out_ref[index] = in_ref[:, index * share : (index + 1) * share]


def split_columns(array, pieces):
    rows, width = array.shape
    share = width // pieces
    some = pieces // 2
    return pl.pallas_call(
        split_kernel,
        grid=(2,),
        in_specs=[pl.BlockSpec((rows, some * share), lambda i: (0, i))],
        out_specs=pl.BlockSpec((some, rows, share), lambda i: (i, 0, 0)),
        out_shape=jax.ShapeDtypeStruct((pieces, rows, share), array.dtype),
        compiler_params=pltpu.CompilerParams(vmem_limit_bytes=SCOPED),
        cost_estimate=pl.CostEstimate(flops=0, bytes_accessed=4 * rows * width, transcendentals=0),
        name="split_columns",
    )(array)


def shared_kernel(latent_ref, up_ref, key_ref, value_ref, doc_col_ref, doc_row_ref):
    @pl.when(pl.program_id(0) == 0)
    def _():
        extra = latent_ref[:, KV_RANK:].astype(jnp.float32)
        doc_col_ref[...] = extra[:, ROPE : ROPE + 1]
        doc_row_ref[...] = extra.T[ROPE : ROPE + 1, :]

    key_values = jnp.dot(latent_ref[:, :KV_RANK], up_ref[...], preferred_element_type=jnp.float32)
    tail = latent_ref[:, KV_RANK:].astype(jnp.float32)
    tail = jnp.where(lax.broadcasted_iota(jnp.int32, tail.shape, 1) < ROPE, tail, 0.0)
    wide = NOPE + VDIM
    key_ref[:, :256] = jnp.concatenate([key_values[:, :NOPE], tail], axis=1).astype(jnp.bfloat16)
    second = jnp.concatenate([key_values[:, wide : wide + NOPE], tail], axis=1)
    key_ref[:, 256:] = pltpu.roll(second, ROPE, 1).astype(jnp.bfloat16)
    value_ref[:, :VDIM] = key_values[:, NOPE:wide].astype(jnp.bfloat16)
    value_ref[:, VDIM : 2 * VDIM] = jnp.ones((value_ref.shape[0], VDIM), jnp.bfloat16)
    value_ref[:, 2 * VDIM :] = key_values[:, wide + NOPE :].astype(jnp.bfloat16)


def keys_and_values(latent, up):
    length = latent.shape[0]
    pairs = up.shape[1] // 512
    return pl.pallas_call(
        shared_kernel,
        grid=(pairs,),
        out_shape=[
            jax.ShapeDtypeStruct((length, pairs * 512), jnp.bfloat16),
            jax.ShapeDtypeStruct((length, pairs * 384), jnp.bfloat16),
            jax.ShapeDtypeStruct((length, 1), jnp.float32),
            jax.ShapeDtypeStruct((1, length), jnp.float32),
        ],
        in_specs=[
            pl.BlockSpec((length, PACKED), lambda i: (0, 0)),
            pl.BlockSpec((KV_RANK, 512), lambda i: (0, i)),
        ],
        out_specs=[
            pl.BlockSpec((length, 512), lambda i: (0, i)),
            pl.BlockSpec((length, 384), lambda i: (0, i)),
            pl.BlockSpec((length, 1), lambda i: (0, 0)),
            pl.BlockSpec((1, length), lambda i: (0, 0)),
        ],
        compiler_params=pltpu.CompilerParams(vmem_limit_bytes=LARGE),
        cost_estimate=pl.CostEstimate(flops=2 * length * KV_RANK * 512 * pairs, bytes_accessed=12 << 20, transcendentals=0),
        name="keys_and_values",
    )(latent, up)


def attend_kernel(windows, where_ref, q_ref, key_ref, value_ref, doc_col_ref, doc_row_ref, out_ref, bias_ref):
    @pl.when(pl.program_id(0) == 0)
    def _():
        for index, (start, first, end) in enumerate(windows):
            shape = (QUERY_BLOCK, end - first)
            query_pos = start + lax.broadcasted_iota(jnp.int32, shape, 0)
            key_pos = first + lax.broadcasted_iota(jnp.int32, shape, 1)
            same = doc_col_ref[start : start + QUERY_BLOCK, :] == doc_row_ref[:, first:end]
            bias_ref[index, :, : end - first] = jnp.where((key_pos <= query_pos) & same, 0.0, MASKED)

    scale = (NOPE + ROPE) ** (-0.5) * LOG2_E
    for index, (start, first, end) in enumerate(windows):
        for head in range(2):
            queries = q_ref[start : start + QUERY_BLOCK, head * 128 : head * 128 + 256]
            scores = lax.dot_general(
                queries,
                key_ref[first:end, head * 256 : head * 256 + 256],
                (((1,), (1,)), ((), ())),
                preferred_element_type=jnp.float32,
            )
            scores = scores * scale + bias_ref[index, :, : end - first]
            peak = jnp.max(scores, axis=-1, keepdims=True)
            weights = jnp.exp2(scores - peak).astype(jnp.bfloat16)
            mixed = jnp.dot(
                weights, value_ref[first:end, head * 128 : head * 128 + 256], preferred_element_type=jnp.float32
            )
            low, high = mixed[:, :VDIM], mixed[:, VDIM:]
            result = (low / high if head == 0 else high / low).astype(jnp.bfloat16)
            half = QUERY_BLOCK // 2
            for side in range(2):
                mine = where_ref[0] == side
                turn = 1 - 2 * side
                step = lax.rem((where_ref[1] - index) * turn + 8, 4)
                block = jnp.where(mine, lax.rem(step + 3, 4), 4 + step)
                place = pl.ds(pl.multiple_of(block * half, half), half)
                out_ref[place, head * VDIM : (head + 1) * VDIM] = result[side * half : (side + 1) * half]


def attend(where, head_queries, keys, values, doc_col, doc_row):
    length, width = head_queries.shape
    pairs = width // 384
    windows = key_windows(length)
    widest = max(end - first for _, first, end in windows)
    return pl.pallas_call(
        lambda *refs: attend_kernel(windows, *refs),
        grid_spec=pltpu.PrefetchScalarGridSpec(
            num_scalar_prefetch=1,
            grid=(pairs,),
            in_specs=[
                pl.BlockSpec((length, 384), lambda i, w: (0, i)),
                pl.BlockSpec((length, 512), lambda i, w: (0, i)),
                pl.BlockSpec((length, 384), lambda i, w: (0, i)),
                pl.BlockSpec((length, 1), lambda i, w: (0, 0)),
                pl.BlockSpec((1, length), lambda i, w: (0, 0)),
            ],
            out_specs=pl.BlockSpec((length, 256), lambda i, w: (0, i)),
            scratch_shapes=[pltpu.VMEM((len(windows), QUERY_BLOCK, widest), jnp.float32)],
        ),
        out_shape=jax.ShapeDtypeStruct((length, pairs * 256), jnp.bfloat16),
        compiler_params=pltpu.CompilerParams(vmem_limit_bytes=LARGE),
        cost_estimate=pl.CostEstimate(flops=10**8, bytes_accessed=1 << 20, transcendentals=10**5),
        name="attend",
    )(where, head_queries, keys, values, doc_col, doc_row)


def gate_up_kernel(first, last, width, where_ref, *refs):
    blocks = refs[:5]
    gain_ref, weight_ref = refs[5:7]
    rest = refs[7:]
    scaled_ref = rest[-1]
    squares = []
    rows, depth = blocks[0].shape
    for index, parts in enumerate(((blocks[0],), (blocks[1],), blocks[2:4], (blocks[4],))):
        square = jnp.zeros((rows, 1), jnp.float32)
        column = 0
        for part in parts:
            values = part[...].astype(jnp.float32)
            square = square + jnp.sum(values * values, axis=-1, keepdims=True)
            span = slice(column, column + values.shape[1])
            scaled = (values * gain_ref[:, span]).astype(jnp.bfloat16)
            scaled_ref[index * rows : (index + 1) * rows, span] = scaled
            column += values.shape[1]
        squares.append(square)
    product = lax.dot_general(
        scaled_ref[...], weight_ref[...], (((1,), (1,)), ((), ())), preferred_element_type=jnp.float32
    )
    square = jnp.concatenate(squares, axis=0)
    out = rest
    if not first:
        product = product + rest[0][...]
        square = square + rest[1][:, :1]
        out = rest[2:]
    if not last:
        out[0][...] = product
        out[1][...] = jnp.broadcast_to(square, (4 * rows, 128))
        return
    product = product * lax.rsqrt(square / width + EPS)
    hidden = product.shape[1] // 2
    gate_proj, up_proj = product[:, :hidden], product[:, hidden:]
    active = (gate_proj / (1.0 + jnp.exp(-gate_proj)) * up_proj).astype(jnp.bfloat16)
    for step in range(4):
        place = lax.rem(where_ref[1] + step, 4)
        out[0][pl.ds(pl.multiple_of(place * rows, rows), rows), :] = active[step * rows : (step + 1) * rows]


def gate_up(where, blocks, gain, weights, earlier, last, width):
    total = 4 * blocks[0].shape[0]
    units, depth = weights.shape
    vmem = pl.BlockSpec(memory_space=pltpu.VMEM)
    if last:
        out_shape = jax.ShapeDtypeStruct((total, units // 2), jnp.bfloat16)
    else:
        out_shape = [
            jax.ShapeDtypeStruct((total, units), jnp.float32),
            jax.ShapeDtypeStruct((total, 128), jnp.float32),
        ]
    return pl.pallas_call(
        lambda *refs: gate_up_kernel(earlier is None, last, width, *refs),
        in_specs=[pl.BlockSpec(memory_space=pltpu.SMEM)] + [vmem] * (len(blocks) + 2 + (0 if earlier is None else 2)),
        out_specs=vmem if last else [vmem] * 2,
        out_shape=out_shape,
        scratch_shapes=[pltpu.VMEM((total, depth), jnp.bfloat16)],
        compiler_params=pltpu.CompilerParams(vmem_limit_bytes=SCOPED),
        cost_estimate=pl.CostEstimate(flops=10**6, bytes_accessed=1 << 16, transcendentals=0),
        name="gate_up",
    )(where, *blocks, gain, weights, *(earlier or ()))


def down_kernel(where_ref, active_ref, *refs):
    parts = refs[:8]
    same_ref, other_ref, out_ref, weight_ref, rows_ref = refs[8:]
    z_count, hidden, _ = same_ref.shape
    units = 2 * hidden

    @pl.when(pl.program_id(0) == 0)
    def _():
        for step in range(z_count):
            chip = pl.ds(lax.rem(where_ref[1] + step, z_count), 1)
            weight_ref[step * units : step * units + hidden, :] = same_ref[chip][0]
            weight_ref[step * units + hidden : (step + 1) * units, :] = other_ref[chip][0]

    count = rows_ref.shape[0]
    rows_ref[:, :units] = active_ref[...]
    for index in range(2):

        @pl.when(pl.program_id(0) == index)
        def _(index=index):
            above_ref, left_ref, right_ref, below_ref = parts[4 * index : 4 * index + 4]
            rows_ref[:, units : 2 * units] = above_ref[...]
            rows_ref[: count // 2, 2 * units : 3 * units] = left_ref[...]
            rows_ref[count // 2 :, 2 * units : 3 * units] = right_ref[...]
            rows_ref[:, 3 * units :] = below_ref[...]

    out_ref[...] = jnp.dot(rows_ref[...], weight_ref[...], preferred_element_type=jnp.float32).astype(jnp.bfloat16)


def down(where, active, parts, same, other):
    total, units = active.shape
    z_count, _, width = same.shape
    count = total // 2
    whole = [pl.BlockSpec(value.shape, lambda i, w: (0, 0)) for value in parts]
    weight_spec = pl.BlockSpec(same.shape, lambda i, w: (0, 0, 0))
    return pl.pallas_call(
        down_kernel,
        grid_spec=pltpu.PrefetchScalarGridSpec(
            num_scalar_prefetch=1,
            grid=(2,),
            in_specs=[pl.BlockSpec((count, units), lambda i, w: (i, 0))] + whole + [weight_spec] * 2,
            out_specs=pl.BlockSpec((count, width), lambda i, w: (i, 0)),
            scratch_shapes=[
                pltpu.VMEM((z_count * units, width), jnp.bfloat16),
                pltpu.VMEM((count, z_count * units), jnp.bfloat16),
            ],
        ),
        out_shape=jax.ShapeDtypeStruct((total, width), jnp.bfloat16),
        compiler_params=pltpu.CompilerParams(vmem_limit_bytes=LARGE // 2),
        cost_estimate=pl.CostEstimate(flops=2 * 10**9, bytes_accessed=6 << 20, transcendentals=0),
        name="down",
    )(where, active, *parts, same, other)


def combine_kernel(high_ref, low_ref, expert_ref, hidden_ref, out_ref):
    count, _, tile = expert_ref.shape
    for index in range(count):
        rows = expert_ref[index]
        moe = jnp.dot(high_ref[...], rows, preferred_element_type=jnp.float32)
        moe = moe + jnp.dot(low_ref[...], rows, preferred_element_type=jnp.float32)
        span = slice(index * tile, (index + 1) * tile)
        out_ref[:, span] = (hidden_ref[:, span].astype(jnp.float32) + moe).astype(jnp.bfloat16)


def combine(high, low, expert_out, hidden):
    rows, width = hidden.shape
    pieces, slots, tile = expert_out.shape
    whole = pl.BlockSpec((rows, slots), lambda i: (0, 0))
    return pl.pallas_call(
        combine_kernel,
        grid=(pieces // 2,),
        in_specs=[
            whole,
            whole,
            pl.BlockSpec((2, slots, tile), lambda i: (i, 0, 0)),
            pl.BlockSpec((rows, 2 * tile), lambda i: (0, i)),
        ],
        out_specs=pl.BlockSpec((rows, 2 * tile), lambda i: (0, i)),
        out_shape=jax.ShapeDtypeStruct((rows, width), jnp.bfloat16),
        cost_estimate=pl.CostEstimate(flops=4 * rows * slots * width, bytes_accessed=4 << 20, transcendentals=0),
        name="combine",
    )(high, low, expert_out, hidden)


def on_device(
    queries,
    latents,
    latent_gain,
    latent_up,
    document_ids,
    output_weights,
    residual,
    norm_gain,
    expert_ids,
    route_gates,
    gate_weights,
    up_weights,
    down_weights,
):
    seq = ("z", "core")
    seq_count = lax.axis_size(seq)
    group_count = lax.axis_size("exp")
    tok_rows = residual.shape[1]
    model_width = residual.shape[2]
    z_count = lax.axis_size("z")
    core, z_place = lax.axis_index("core"), lax.axis_index("z")
    own = jnp.stack([core, z_place]).astype(jnp.int32)
    around = [(i, (i // 2 + 1 - 2 * (i % 2)) % z_count * 2 + i % 2) for i in range(seq_count)]
    reverse = [(i, (i // 2 - 1 + 2 * (i % 2)) % z_count * 2 + i % 2) for i in range(seq_count)]
    above = [(i, (i + 1) % z_count) for i in range(z_count)]
    below = [(i, (i - 1) % z_count) for i in range(z_count)]

    normed = rms_scale(latents[0, :, :KV_RANK].astype(jnp.float32), latent_gain).astype(jnp.bfloat16)
    spare = PACKED - KV_RANK - ROPE - 1
    packed = jnp.concatenate(
        [
            normed,
            latents[0, :, KV_RANK:],
            document_ids[0][:, None].astype(jnp.bfloat16),
            jnp.zeros((tok_rows, spare), jnp.bfloat16),
        ],
        axis=1,
    )
    all_latent = lax.all_gather(packed, seq, axis=0, tiled=True)
    by_head = split_columns(queries[0], seq_count)
    arrived_queries = lax.all_to_all(by_head, seq, split_axis=0, concat_axis=0, tiled=True)
    keys, values, doc_col, doc_row = keys_and_values(all_latent, latent_up)
    head_queries = arrived_queries.reshape(seq_count * tok_rows, -1)

    piece = model_width // z_count
    down_pieces = split_columns(down_weights[0], z_count)
    width = model_width // 2
    spans = [slice(0, width), slice(width, model_width)]
    def across(value):
        return lax.ppermute(value, "core", [(0, 1), (1, 0)])

    others = across(gate_weights[0]), across(up_weights[0])
    halves = []
    for span in spans:
        units = [gate_weights[0, :, span], others[0][:, span], up_weights[0, :, span], others[1][:, span]]
        halves.append(jnp.concatenate(units, axis=0))
    halves, head_queries = lax.optimization_barrier((halves, head_queries))
    down_pieces, keys = lax.optimization_barrier((down_pieces, keys))
    head_queries, keys, values, doc_col, doc_row = lax.optimization_barrier(
        (head_queries, keys, values, doc_col, doc_row)
    )
    down_columns = lax.all_to_all(down_pieces, "z", split_axis=0, concat_axis=0, tiled=True)

    window = jnp.arange(group_count, dtype=jnp.int32) * GROUP_EXPERTS
    matches = expert_ids[0][:, :, None] == window
    chosen = jnp.any(matches, axis=1).astype(jnp.bfloat16)
    gate_share = jnp.sum(jnp.where(matches, route_gates[0][:, :, None], jnp.zeros((), jnp.float32)), axis=1)
    row_ids = jnp.arange(tok_rows, dtype=jnp.int32)
    earlier = (row_ids[None, :] < row_ids[:, None]).astype(jnp.bfloat16)
    slot_rank = jnp.dot(earlier, chosen, preferred_element_type=jnp.float32)
    slot_ids = jnp.arange(CAP, dtype=jnp.float32)
    slot_picks = chosen.astype(jnp.float32)[:, :, None] * (slot_rank[:, :, None] == slot_ids).astype(jnp.float32)
    slot_picks = slot_picks.reshape(tok_rows, group_count * CAP)
    mixing = slot_picks * jnp.repeat(gate_share, CAP, axis=1)
    picks = slot_picks.astype(jnp.bfloat16)

    high = mixing.astype(jnp.bfloat16)
    low = (mixing - high.astype(jnp.float32)).astype(jnp.bfloat16)
    head_queries, picks, high, low = lax.optimization_barrier((head_queries, picks, high, low))
    head_out = attend(own, head_queries, keys, values, doc_col, doc_row)
    gain = norm_gain[None, :]
    half = head_out.shape[0] // 2

    def up(value):
        return lax.ppermute(value, "z", above)

    def down_one(value):
        return lax.ppermute(value, "z", below)

    def turn_round(value):
        return lax.ppermute(value, seq, around)

    def turn_back(value):
        return lax.ppermute(value, seq, reverse)

    def together(*arrays):
        return lax.optimization_barrier(arrays)

    def project(span):
        product = jnp.dot(head_out, output_weights[:, span], preferred_element_type=jnp.float32).astype(jnp.bfloat16)
        mine, theirs = together(product[:half], product[half:])
        return mine.reshape(z_count, tok_rows, width), theirs.reshape(z_count, tok_rows, width)

    left, right = slice(0, width // 2), slice(width // 2, width)

    def add(arrived, mine, added, step):
        total = arrived.astype(jnp.float32) + mine[(step + 3) % 4].astype(jnp.float32)
        return total + added[step].astype(jnp.float32)

    def dispatch(total, span):
        stage_hidden = (residual[0, :, span].astype(jnp.float32) + total).astype(jnp.bfloat16)
        outgoing = jnp.einsum("ts,td->sd", picks, stage_hidden, preferred_element_type=jnp.float32).astype(jnp.bfloat16)
        arrived = lax.all_to_all(
            outgoing.reshape(group_count, CAP, -1), "exp", split_axis=0, concat_axis=0, tiled=True
        ).reshape(group_count * CAP, -1)
        return stage_hidden, arrived

    mine_a, theirs_a = project(spans[0])
    theirs_a, down_columns = together(theirs_a, down_columns)
    added_a = across(theirs_a)
    run_a = mine_a[0] + added_a[1]
    head_out, run_a = together(head_out, run_a)
    mine_b, theirs_b = project(spans[1])
    run_a = add(turn_round(run_a), mine_a, added_a, 2).astype(jnp.bfloat16)
    theirs_b, run_a = together(theirs_b, run_a)
    added_b = across(theirs_b)
    run_b = mine_b[2] + added_b[3]
    run_b, down_columns = together(run_b, down_columns)
    down_other = across(down_columns)
    run_a = add(turn_round(run_a), mine_a, added_a, 3).astype(jnp.bfloat16)
    run_b = add(turn_back(run_b), mine_b, added_b, 2).astype(jnp.bfloat16)
    hidden_a, early = dispatch(add(turn_round(run_a), mine_a, added_a, 0), spans[0])
    run_b = add(turn_back(run_b), mine_b, added_b, 1).astype(jnp.bfloat16)
    last_b = turn_back(run_b)
    last_b, early, down_other = together(last_b, early, down_other)
    hidden_b, late = dispatch(add(last_b, mine_b, added_b, 0), spans[1])
    hidden = [hidden_a, hidden_b]

    def gather(value, cut, more):
        from_above, from_below, *more = together(down_one(value), up(value), *more)
        return [from_above, up(from_below[cut[0]]), down_one(from_above[cut[1]]), from_below], more

    columns = (slice(None), left), (slice(None), right)
    blocks, (late,) = gather(early, columns, [late])
    carried = gate_up(own, [early] + blocks, gain[:, spans[0]], halves[0], None, False, model_width)
    blocks, _ = gather(late, columns, [])
    blocks[1], blocks[2], *carried = together(blocks[1], blocks[2], *carried)
    active = gate_up(own, [late] + blocks, gain[:, spans[1]], halves[1], carried, True, model_width)
    middle = active.shape[0] // 2
    quarter = middle // 2
    parts = []
    for rows in (slice(0, middle), slice(middle, None)):
        parts += gather(active[rows], (slice(0, quarter), slice(quarter, None)), [])[0]
    results = down(own, active, parts, down_columns, down_other)
    results = results.reshape(z_count * group_count, CAP, piece)
    returned = lax.all_to_all(results, ("z", "exp"), split_axis=0, concat_axis=0, tiled=True)
    returned = returned.reshape(z_count, group_count * CAP, piece)
    return combine(high, low, returned, jnp.concatenate(hidden, axis=1))[None]


def solution(mesh):
    mesh = jax.sharding.Mesh(mesh.devices.reshape(-1, 2, mesh.shape["exp"]), ("z", "core", "exp"))
    return jax.shard_map(
        on_device,
        mesh=mesh,
        in_specs=(
            P("exp", ("z", "core"), None),
            P("exp", ("z", "core"), None),
            P(),
            P(None, ("z", "core")),
            P("exp", ("z", "core")),
            P(("z", "core"), None),
            P("exp", ("z", "core"), None),
            P(),
            P("exp", ("z", "core"), None),
            P("exp", ("z", "core"), None),
            P("exp", ("z", "core"), None),
            P("exp", ("z", "core"), None),
            P("exp", ("z", "core"), None),
        ),
        out_specs=P("exp", ("z", "core"), None),
        check_vma=False,
    )
```

```python
import jax
import jax.numpy as jnp
from jax import lax
from jax.experimental import pallas as pl
from jax.experimental.pallas import tpu as pltpu
from jax.sharding import PartitionSpec as P

NOPE = 128
ROPE = 64
VDIM = 128
KV_RANK = 512
GROUP_EXPERTS = 10
CAP = 8
DOC_MAX = 512
QUERY_BLOCK = 256
PACKED = 640
SCOPED = 24 << 20
LARGE = 58 << 20


EPS = 1e-06
MASKED = -1e30
LOG2_E = 1.4426950408889634


def rms_scale(values, gain):
    mean_sq = jnp.mean(values * values, axis=-1, keepdims=True)
    return values * lax.rsqrt(mean_sq + EPS) * gain


def key_windows(length):
    windows = []
    for start in range(0, length, QUERY_BLOCK):
        first = max(0, start - DOC_MAX + 1) // QUERY_BLOCK * QUERY_BLOCK
        windows.append((start, first, start + QUERY_BLOCK))
    return windows


def split_kernel(in_ref, out_ref):
    pieces, _, share = out_ref.shape
    for index in range(pieces):
        out_ref[index] = in_ref[:, index * share : (index + 1) * share]


def split_columns(array, pieces):
    rows, width = array.shape
    share = width // pieces
    some = pieces // 2
    return pl.pallas_call(
        split_kernel,
        grid=(2,),
        in_specs=[pl.BlockSpec((rows, some * share), lambda i: (0, i))],
        out_specs=pl.BlockSpec((some, rows, share), lambda i: (i, 0, 0)),
        out_shape=jax.ShapeDtypeStruct((pieces, rows, share), array.dtype),
        compiler_params=pltpu.CompilerParams(vmem_limit_bytes=SCOPED),
        cost_estimate=pl.CostEstimate(flops=0, bytes_accessed=4 * rows * width, transcendentals=0),
        name="split_columns",
    )(array)


def shared_kernel(latent_ref, up_ref, key_ref, value_ref, doc_col_ref, doc_row_ref):
    @pl.when(pl.program_id(0) == 0)
    def _():
        extra = latent_ref[:, KV_RANK:].astype(jnp.float32)
        doc_col_ref[...] = extra[:, ROPE : ROPE + 1]
        doc_row_ref[...] = extra.T[ROPE : ROPE + 1, :]

    key_values = jnp.dot(latent_ref[:, :KV_RANK], up_ref[...], preferred_element_type=jnp.float32)
    tail = latent_ref[:, KV_RANK:].astype(jnp.float32)
    tail = jnp.where(lax.broadcasted_iota(jnp.int32, tail.shape, 1) < ROPE, tail, 0.0)
    wide = NOPE + VDIM
    key_ref[:, :256] = jnp.concatenate([key_values[:, :NOPE], tail], axis=1).astype(jnp.bfloat16)
    second = jnp.concatenate([key_values[:, wide : wide + NOPE], tail], axis=1)
    key_ref[:, 256:] = pltpu.roll(second, ROPE, 1).astype(jnp.bfloat16)
    value_ref[:, :VDIM] = key_values[:, NOPE:wide].astype(jnp.bfloat16)
    value_ref[:, VDIM : 2 * VDIM] = jnp.ones((value_ref.shape[0], VDIM), jnp.bfloat16)
    value_ref[:, 2 * VDIM :] = key_values[:, wide + NOPE :].astype(jnp.bfloat16)


def keys_and_values(latent, up):
    length = latent.shape[0]
    pairs = up.shape[1] // 512
    return pl.pallas_call(
        shared_kernel,
        grid=(pairs,),
        out_shape=[
            jax.ShapeDtypeStruct((length, pairs * 512), jnp.bfloat16),
            jax.ShapeDtypeStruct((length, pairs * 384), jnp.bfloat16),
            jax.ShapeDtypeStruct((length, 1), jnp.float32),
            jax.ShapeDtypeStruct((1, length), jnp.float32),
        ],
        in_specs=[
            pl.BlockSpec((length, PACKED), lambda i: (0, 0)),
            pl.BlockSpec((KV_RANK, 512), lambda i: (0, i)),
        ],
        out_specs=[
            pl.BlockSpec((length, 512), lambda i: (0, i)),
            pl.BlockSpec((length, 384), lambda i: (0, i)),
            pl.BlockSpec((length, 1), lambda i: (0, 0)),
            pl.BlockSpec((1, length), lambda i: (0, 0)),
        ],
        compiler_params=pltpu.CompilerParams(vmem_limit_bytes=LARGE),
        cost_estimate=pl.CostEstimate(flops=2 * length * KV_RANK * 512 * pairs, bytes_accessed=12 << 20, transcendentals=0),
        name="keys_and_values",
    )(latent, up)


def attend_kernel(windows, where_ref, q_ref, key_ref, value_ref, doc_col_ref, doc_row_ref, out_ref, bias_ref):
    @pl.when(pl.program_id(0) == 0)
    def _():
        for index, (start, first, end) in enumerate(windows):
            shape = (QUERY_BLOCK, end - first)
            query_pos = start + lax.broadcasted_iota(jnp.int32, shape, 0)
            key_pos = first + lax.broadcasted_iota(jnp.int32, shape, 1)
            same = doc_col_ref[start : start + QUERY_BLOCK, :] == doc_row_ref[:, first:end]
            bias_ref[index, :, : end - first] = jnp.where((key_pos <= query_pos) & same, 0.0, MASKED)

    scale = (NOPE + ROPE) ** (-0.5) * LOG2_E
    for index, (start, first, end) in enumerate(windows):
        for head in range(2):
            queries = q_ref[start : start + QUERY_BLOCK, head * 128 : head * 128 + 256]
            scores = lax.dot_general(
                queries,
                key_ref[first:end, head * 256 : head * 256 + 256],
                (((1,), (1,)), ((), ())),
                preferred_element_type=jnp.float32,
            )
            scores = scores * scale + bias_ref[index, :, : end - first]
            peak = jnp.max(scores, axis=-1, keepdims=True)
            weights = jnp.exp2(scores - peak).astype(jnp.bfloat16)
            mixed = jnp.dot(
                weights, value_ref[first:end, head * 128 : head * 128 + 256], preferred_element_type=jnp.float32
            )
            low, high = mixed[:, :VDIM], mixed[:, VDIM:]
            result = (low / high if head == 0 else high / low).astype(jnp.bfloat16)
            half = QUERY_BLOCK // 2
            for side in range(2):
                mine = where_ref[0] == side
                turn = 1 - 2 * side
                step = lax.rem((where_ref[1] - index) * turn + 8, 4)
                block = jnp.where(mine, lax.rem(step + 3, 4), 4 + step)
                place = pl.ds(pl.multiple_of(block * half, half), half)
                out_ref[place, head * VDIM : (head + 1) * VDIM] = result[side * half : (side + 1) * half]


def attend(where, head_queries, keys, values, doc_col, doc_row):
    length, width = head_queries.shape
    pairs = width // 384
    windows = key_windows(length)
    widest = max(end - first for _, first, end in windows)
    return pl.pallas_call(
        lambda *refs: attend_kernel(windows, *refs),
        grid_spec=pltpu.PrefetchScalarGridSpec(
            num_scalar_prefetch=1,
            grid=(pairs,),
            in_specs=[
                pl.BlockSpec((length, 384), lambda i, w: (0, i)),
                pl.BlockSpec((length, 512), lambda i, w: (0, i)),
                pl.BlockSpec((length, 384), lambda i, w: (0, i)),
                pl.BlockSpec((length, 1), lambda i, w: (0, 0)),
                pl.BlockSpec((1, length), lambda i, w: (0, 0)),
            ],
            out_specs=pl.BlockSpec((length, 256), lambda i, w: (0, i)),
            scratch_shapes=[pltpu.VMEM((len(windows), QUERY_BLOCK, widest), jnp.float32)],
        ),
        out_shape=jax.ShapeDtypeStruct((length, pairs * 256), jnp.bfloat16),
        compiler_params=pltpu.CompilerParams(vmem_limit_bytes=LARGE),
        cost_estimate=pl.CostEstimate(flops=10**8, bytes_accessed=1 << 20, transcendentals=10**5),
        name="attend",
    )(where, head_queries, keys, values, doc_col, doc_row)


def gate_up_kernel(first, last, width, where_ref, *refs):
    blocks = refs[:5]
    gain_ref, weight_ref = refs[5:7]
    rest = refs[7:]
    scaled_ref = rest[-1]
    squares = []
    rows, depth = blocks[0].shape
    for index, parts in enumerate(((blocks[0],), (blocks[1],), blocks[2:4], (blocks[4],))):
        square = jnp.zeros((rows, 1), jnp.float32)
        column = 0
        for part in parts:
            values = part[...].astype(jnp.float32)
            square = square + jnp.sum(values * values, axis=-1, keepdims=True)
            span = slice(column, column + values.shape[1])
            scaled = (values * gain_ref[:, span]).astype(jnp.bfloat16)
            scaled_ref[index * rows : (index + 1) * rows, span] = scaled
            column += values.shape[1]
        squares.append(square)
    product = lax.dot_general(
        scaled_ref[...], weight_ref[...], (((1,), (1,)), ((), ())), preferred_element_type=jnp.float32
    )
    square = jnp.concatenate(squares, axis=0)
    out = rest
    if not first:
        product = product + rest[0][...]
        square = square + rest[1][:, :1]
        out = rest[2:]
    if not last:
        out[0][...] = product
        out[1][...] = jnp.broadcast_to(square, (4 * rows, 128))
        return
    product = product * lax.rsqrt(square / width + EPS)
    hidden = product.shape[1] // 2
    gate_proj, up_proj = product[:, :hidden], product[:, hidden:]
    active = (gate_proj / (1.0 + jnp.exp(-gate_proj)) * up_proj).astype(jnp.bfloat16)
    for step in range(4):
        place = lax.rem(where_ref[1] + step, 4)
        out[0][pl.ds(pl.multiple_of(place * rows, rows), rows), :] = active[step * rows : (step + 1) * rows]


def gate_up(where, blocks, gain, weights, earlier, last, width):
    total = 4 * blocks[0].shape[0]
    units, depth = weights.shape
    vmem = pl.BlockSpec(memory_space=pltpu.VMEM)
    if last:
        out_shape = jax.ShapeDtypeStruct((total, units // 2), jnp.bfloat16)
    else:
        out_shape = [
            jax.ShapeDtypeStruct((total, units), jnp.float32),
            jax.ShapeDtypeStruct((total, 128), jnp.float32),
        ]
    return pl.pallas_call(
        lambda *refs: gate_up_kernel(earlier is None, last, width, *refs),
        in_specs=[pl.BlockSpec(memory_space=pltpu.SMEM)] + [vmem] * (len(blocks) + 2 + (0 if earlier is None else 2)),
        out_specs=vmem if last else [vmem] * 2,
        out_shape=out_shape,
        scratch_shapes=[pltpu.VMEM((total, depth), jnp.bfloat16)],
        compiler_params=pltpu.CompilerParams(vmem_limit_bytes=SCOPED),
        cost_estimate=pl.CostEstimate(flops=10**6, bytes_accessed=1 << 16, transcendentals=0),
        name="gate_up",
    )(where, *blocks, gain, weights, *(earlier or ()))


def down_kernel(where_ref, active_ref, *refs):
    parts = refs[:4]
    same_ref, other_ref, out_ref, weight_ref, rows_ref = refs[4:]
    z_count, hidden, _ = same_ref.shape
    units = 2 * hidden
    total = active_ref.shape[0]
    for step in range(z_count):
        chip = pl.ds(lax.rem(where_ref[1] + step, z_count), 1)
        weight_ref[step * units : step * units + hidden, :] = same_ref[chip][0]
        weight_ref[step * units + hidden : (step + 1) * units, :] = other_ref[chip][0]
    rows_ref[:, :units] = active_ref[...]
    rows_ref[:, units : 2 * units] = parts[0][...]
    rows_ref[: total // 2, 2 * units : 3 * units] = parts[1][...]
    rows_ref[total // 2 :, 2 * units : 3 * units] = parts[2][...]
    rows_ref[:, 3 * units :] = parts[-1][...]
    half = total // 2
    for start in (0, half):
        product = jnp.dot(rows_ref[start : start + half, :], weight_ref[...], preferred_element_type=jnp.float32)
        out_ref[start : start + half, :] = product.astype(jnp.bfloat16)


def down(where, active, parts, same, other):
    total, units = active.shape
    z_count, _, width = same.shape
    vmem = pl.BlockSpec(memory_space=pltpu.VMEM)
    return pl.pallas_call(
        down_kernel,
        in_specs=[pl.BlockSpec(memory_space=pltpu.SMEM)] + [vmem] * (len(parts) + 3),
        out_specs=vmem,
        scratch_shapes=[
            pltpu.VMEM((z_count * units, width), jnp.bfloat16),
            pltpu.VMEM((total, z_count * units), jnp.bfloat16),
        ],
        out_shape=jax.ShapeDtypeStruct((total, width), jnp.bfloat16),
        compiler_params=pltpu.CompilerParams(vmem_limit_bytes=LARGE // 2),
        cost_estimate=pl.CostEstimate(flops=2 * 10**9, bytes_accessed=6 << 20, transcendentals=0),
        name="down",
    )(where, active, *parts, same, other)


def combine_kernel(high_ref, low_ref, expert_ref, hidden_ref, out_ref):
    count, _, tile = expert_ref.shape
    for index in range(count):
        rows = expert_ref[index]
        moe = jnp.dot(high_ref[...], rows, preferred_element_type=jnp.float32)
        moe = moe + jnp.dot(low_ref[...], rows, preferred_element_type=jnp.float32)
        span = slice(index * tile, (index + 1) * tile)
        out_ref[:, span] = (hidden_ref[:, span].astype(jnp.float32) + moe).astype(jnp.bfloat16)


def combine(high, low, expert_out, hidden):
    rows, width = hidden.shape
    pieces, slots, tile = expert_out.shape
    whole = pl.BlockSpec((rows, slots), lambda i: (0, 0))
    return pl.pallas_call(
        combine_kernel,
        grid=(pieces // 2,),
        in_specs=[
            whole,
            whole,
            pl.BlockSpec((2, slots, tile), lambda i: (i, 0, 0)),
            pl.BlockSpec((rows, 2 * tile), lambda i: (0, i)),
        ],
        out_specs=pl.BlockSpec((rows, 2 * tile), lambda i: (0, i)),
        out_shape=jax.ShapeDtypeStruct((rows, width), jnp.bfloat16),
        cost_estimate=pl.CostEstimate(flops=4 * rows * slots * width, bytes_accessed=4 << 20, transcendentals=0),
        name="combine",
    )(high, low, expert_out, hidden)


def on_device(
    queries,
    latents,
    latent_gain,
    latent_up,
    document_ids,
    output_weights,
    residual,
    norm_gain,
    expert_ids,
    route_gates,
    gate_weights,
    up_weights,
    down_weights,
):
    seq = ("z", "core")
    seq_count = lax.axis_size(seq)
    group_count = lax.axis_size("exp")
    tok_rows = residual.shape[1]
    model_width = residual.shape[2]
    z_count = lax.axis_size("z")
    core, z_place = lax.axis_index("core"), lax.axis_index("z")
    own = jnp.stack([core, z_place]).astype(jnp.int32)
    around = [(i, (i // 2 + 1 - 2 * (i % 2)) % z_count * 2 + i % 2) for i in range(seq_count)]
    reverse = [(i, (i // 2 - 1 + 2 * (i % 2)) % z_count * 2 + i % 2) for i in range(seq_count)]
    above = [(i, (i + 1) % z_count) for i in range(z_count)]
    below = [(i, (i - 1) % z_count) for i in range(z_count)]

    normed = rms_scale(latents[0, :, :KV_RANK].astype(jnp.float32), latent_gain).astype(jnp.bfloat16)
    spare = PACKED - KV_RANK - ROPE - 1
    packed = jnp.concatenate(
        [
            normed,
            latents[0, :, KV_RANK:],
            document_ids[0][:, None].astype(jnp.bfloat16),
            jnp.zeros((tok_rows, spare), jnp.bfloat16),
        ],
        axis=1,
    )
    all_latent = lax.all_gather(packed, seq, axis=0, tiled=True)
    by_head = split_columns(queries[0], seq_count)
    arrived_queries = lax.all_to_all(by_head, seq, split_axis=0, concat_axis=0, tiled=True)
    keys, values, doc_col, doc_row = keys_and_values(all_latent, latent_up)
    head_queries = arrived_queries.reshape(seq_count * tok_rows, -1)

    piece = model_width // z_count
    down_pieces = split_columns(down_weights[0], z_count)
    width = model_width // 2
    spans = [slice(0, width), slice(width, model_width)]
    def across(value):
        return lax.ppermute(value, "core", [(0, 1), (1, 0)])

    others = across(gate_weights[0]), across(up_weights[0])
    halves = []
    for span in spans:
        units = [gate_weights[0, :, span], others[0][:, span], up_weights[0, :, span], others[1][:, span]]
        halves.append(jnp.concatenate(units, axis=0))
    halves, head_queries = lax.optimization_barrier((halves, head_queries))
    down_pieces, keys = lax.optimization_barrier((down_pieces, keys))
    head_queries, keys, values, doc_col, doc_row = lax.optimization_barrier(
        (head_queries, keys, values, doc_col, doc_row)
    )
    down_columns = lax.all_to_all(down_pieces, "z", split_axis=0, concat_axis=0, tiled=True)

    window = jnp.arange(group_count, dtype=jnp.int32) * GROUP_EXPERTS
    matches = expert_ids[0][:, :, None] == window
    chosen = jnp.any(matches, axis=1).astype(jnp.bfloat16)
    gate_share = jnp.sum(jnp.where(matches, route_gates[0][:, :, None], jnp.zeros((), jnp.float32)), axis=1)
    row_ids = jnp.arange(tok_rows, dtype=jnp.int32)
    earlier = (row_ids[None, :] < row_ids[:, None]).astype(jnp.bfloat16)
    slot_rank = jnp.dot(earlier, chosen, preferred_element_type=jnp.float32)
    slot_ids = jnp.arange(CAP, dtype=jnp.float32)
    slot_picks = chosen.astype(jnp.float32)[:, :, None] * (slot_rank[:, :, None] == slot_ids).astype(jnp.float32)
    slot_picks = slot_picks.reshape(tok_rows, group_count * CAP)
    mixing = slot_picks * jnp.repeat(gate_share, CAP, axis=1)
    picks = slot_picks.astype(jnp.bfloat16)

    high = mixing.astype(jnp.bfloat16)
    low = (mixing - high.astype(jnp.float32)).astype(jnp.bfloat16)
    head_queries, picks, high, low = lax.optimization_barrier((head_queries, picks, high, low))
    head_out = attend(own, head_queries, keys, values, doc_col, doc_row)
    gain = norm_gain[None, :]
    half = head_out.shape[0] // 2

    def up(value):
        return lax.ppermute(value, "z", above)

    def down_one(value):
        return lax.ppermute(value, "z", below)

    def turn_round(value):
        return lax.ppermute(value, seq, around)

    def turn_back(value):
        return lax.ppermute(value, seq, reverse)

    def together(*arrays):
        return lax.optimization_barrier(arrays)

    def project(span):
        product = jnp.dot(head_out, output_weights[:, span], preferred_element_type=jnp.float32).astype(jnp.bfloat16)
        mine, theirs = together(product[:half], product[half:])
        return mine.reshape(z_count, tok_rows, width), theirs.reshape(z_count, tok_rows, width)

    left, right = slice(0, width // 2), slice(width // 2, width)

    def add(arrived, mine, added, step):
        total = arrived.astype(jnp.float32) + mine[(step + 3) % 4].astype(jnp.float32)
        return total + added[step].astype(jnp.float32)

    def dispatch(total, span):
        stage_hidden = (residual[0, :, span].astype(jnp.float32) + total).astype(jnp.bfloat16)
        outgoing = jnp.einsum("ts,td->sd", picks, stage_hidden, preferred_element_type=jnp.float32).astype(jnp.bfloat16)
        arrived = lax.all_to_all(
            outgoing.reshape(group_count, CAP, -1), "exp", split_axis=0, concat_axis=0, tiled=True
        ).reshape(group_count * CAP, -1)
        return stage_hidden, arrived

    mine_a, theirs_a = project(spans[0])
    theirs_a, down_columns = together(theirs_a, down_columns)
    added_a = across(theirs_a)
    run_a = mine_a[0] + added_a[1]
    head_out, run_a = together(head_out, run_a)
    mine_b, theirs_b = project(spans[1])
    run_a = add(turn_round(run_a), mine_a, added_a, 2).astype(jnp.bfloat16)
    theirs_b, run_a = together(theirs_b, run_a)
    added_b = across(theirs_b)
    run_b = mine_b[2] + added_b[3]
    run_b, down_columns = together(run_b, down_columns)
    down_other = across(down_columns)
    run_a = add(turn_round(run_a), mine_a, added_a, 3).astype(jnp.bfloat16)
    run_b = add(turn_back(run_b), mine_b, added_b, 2).astype(jnp.bfloat16)
    hidden_a, early = dispatch(add(turn_round(run_a), mine_a, added_a, 0), spans[0])
    run_b = add(turn_back(run_b), mine_b, added_b, 1).astype(jnp.bfloat16)
    last_b = turn_back(run_b)
    last_b, early, down_other = together(last_b, early, down_other)
    hidden_b, late = dispatch(add(last_b, mine_b, added_b, 0), spans[1])
    hidden = [hidden_a, hidden_b]

    def gather(value, cut, more):
        from_above, from_below, *more = together(down_one(value), up(value), *more)
        return [from_above, up(from_below[cut[0]]), down_one(from_above[cut[1]]), from_below], more

    columns = (slice(None), left), (slice(None), right)
    blocks, (late,) = gather(early, columns, [late])
    carried = gate_up(own, [early] + blocks, gain[:, spans[0]], halves[0], None, False, model_width)
    blocks, _ = gather(late, columns, [])
    blocks[1], blocks[2], *carried = together(blocks[1], blocks[2], *carried)
    active = gate_up(own, [late] + blocks, gain[:, spans[1]], halves[1], carried, True, model_width)
    middle = active.shape[0] // 2
    parts, _ = gather(active, (slice(0, middle), slice(middle, None)), [])
    results = down(own, active, parts, down_columns, down_other)
    results = results.reshape(z_count * group_count, CAP, piece)
    returned = lax.all_to_all(results, ("z", "exp"), split_axis=0, concat_axis=0, tiled=True)
    returned = returned.reshape(z_count, group_count * CAP, piece)
    return combine(high, low, returned, jnp.concatenate(hidden, axis=1))[None]


def solution(mesh):
    mesh = jax.sharding.Mesh(mesh.devices.reshape(-1, 2, mesh.shape["exp"]), ("z", "core", "exp"))
    return jax.shard_map(
        on_device,
        mesh=mesh,
        in_specs=(
            P("exp", ("z", "core"), None),
            P("exp", ("z", "core"), None),
            P(),
            P(None, ("z", "core")),
            P("exp", ("z", "core")),
            P(("z", "core"), None),
            P("exp", ("z", "core"), None),
            P(),
            P("exp", ("z", "core"), None),
            P("exp", ("z", "core"), None),
            P("exp", ("z", "core"), None),
            P("exp", ("z", "core"), None),
            P("exp", ("z", "core"), None),
        ),
        out_specs=P("exp", ("z", "core"), None),
        check_vma=False,
    )
```
